32 devices in a mesh: fsdp: 8 (over y, x, core), ctx: 4 (over z).
Axes of the slice: x: 2, y: 2, z: 4, core: 2. Of those that a mesh axis runs over, the one named last changes fastest.
Arguments:
- inputs: bfloat16 [2, 8192, 2048], P(None, ('fsdp', 'ctx')), may hold values from -6 to 6
- depths: int32 [2, 8192], P(None, ('fsdp', 'ctx')), may hold values from 0 to 767, as said below
- parents: int32 [2, 8, 8], P(None, 'fsdp'), may hold values from 0 to 6, as said below
- layout: int32 [2, 8, 8], P(None, 'fsdp'), may hold values from 0 to 7, as said below
- gain_attn: bfloat16 [2048], P('fsdp'), may hold values from 0.5 to 1.5
- w_query: bfloat16 [2048, 2048], P('fsdp'), may hold values from -0.125 to 0.125
- w_key: bfloat16 [2048, 1024], P('fsdp'), may hold values from -0.125 to 0.125
- w_value: bfloat16 [2048, 1024], P('fsdp'), may hold values from -0.125 to 0.125
- query_gain: bfloat16 [128], P('fsdp'), may hold values from 0.099609375 to 1.8984375
- key_gain: bfloat16 [128], P('fsdp'), may hold values from 0.099609375 to 1.8984375
- w_output: bfloat16 [2048, 2048], P('fsdp'), may hold values from -1 to 1
- gain_ffn: bfloat16 [2048], P('fsdp'), may hold values from 0.5 to 1.5
- w_gate: bfloat16 [2048, 6144], P('fsdp'), may hold values from -0.125 to 0.125
- w_up: bfloat16 [2048, 6144], P('fsdp'), may hold values from -0.125 to 0.125
- w_down: bfloat16 [6144, 2048], P('fsdp'), may hold values from -0.078125 to 0.078125
- cotangent: bfloat16 [2, 8192, 2048], P(None, ('fsdp', 'ctx')), may hold values from -6 to 6
Outputs:
- outputs: bfloat16 [2, 8192, 2048], P(None, ('fsdp', 'ctx'))
- grad_inputs: float32 [2, 8192, 2048], P(None, ('fsdp', 'ctx'))
- grad_gain_attn: float32 [2048], P('fsdp')
- grad_w_query: float32 [2048, 2048], P('fsdp')
- grad_w_key: float32 [2048, 1024], P('fsdp')
- grad_w_value: float32 [2048, 1024], P('fsdp')
- grad_query_gain: float32 [128], P('fsdp')
- grad_key_gain: float32 [128], P('fsdp')
- grad_w_output: float32 [2048, 2048], P('fsdp')
- grad_gain_ffn: float32 [2048], P('fsdp')
- grad_w_gate: float32 [2048, 6144], P('fsdp')
- grad_w_up: float32 [2048, 6144], P('fsdp')
- grad_w_down: float32 [6144, 2048], P('fsdp')
The draws below stay inside these ranges and needn't reach their ends.
Inputs may be any that keep to these rules, and one draw needn't show every extreme that they name: `parents`: for each tree, entry 0 (the root) is 0 and every other entry b is less than b. `layout`: for each tree, each segment appears once. `depths`: A token's depth is 128 times the number of proper ancestors of its segment plus its place within the segment.
All inputs are finite; a program needn't handle non-finite values.
Results may differ from the reference program's by a relative error of at most 0.025.
Values may be sent and summed in bfloat16 or wider, within the bound.
No kernel may reach another device: no remote copies, remote signals or barrier semaphores. Data moves between devices by JAX's collectives and lax.ppermute only.
A program may use at most 576 MiB of HBM per device.

```python
import jax
import jax.numpy as jnp
from jax import lax

D = 2048
QH = 16
KVH = 8
DH = 128
FF = 6144
BLK = 128
MB = 2
TREE_BLOCKS = 8
TREE_TOKENS = 1024
TOKENS = 8192
N_FSDP = 8


def single_tree(key):
    first, second = jax.random.split(key)
    ident = jnp.arange(TREE_BLOCKS, dtype=jnp.int32)
    trunk = TREE_BLOCKS // 2
    raw = jax.random.randint(first, (TREE_BLOCKS,), 0, 1 << 20, dtype=jnp.int32)
    picked = raw % trunk
    parent = jnp.where(ident < trunk, ident - 1, picked)
    parent = jnp.where(ident == 0, 0, parent)
    parent = jnp.where(ident == TREE_BLOCKS - 2, trunk - 1, parent)
    parent = jnp.where(ident == TREE_BLOCKS - 1, TREE_BLOCKS - 2, parent).astype(jnp.int32)

    def deeper(block, level):
        return level.at[block].set(level[parent[block]] + 1)
    level = lax.fori_loop(1, TREE_BLOCKS, deeper, jnp.zeros((TREE_BLOCKS,), jnp.int32))
    order = jax.random.permutation(second, ident).astype(jnp.int32)
    seg_level = level[order]
    token_depth = (seg_level[:, None] * BLK + jnp.arange(BLK, dtype=jnp.int32)[None, :]).reshape(-1)
    return (parent, order, token_depth)


def tree_arrays(key):
    base = jax.random.fold_in(key, 11)
    keys = jax.random.split(base, MB * N_FSDP)
    parent, order, token_depth = jax.vmap(single_tree)(keys)
    return (parent.reshape(MB, N_FSDP, TREE_BLOCKS), order.reshape(MB, N_FSDP, TREE_BLOCKS), token_depth.reshape(MB, N_FSDP * TREE_BLOCKS * BLK))


def draw_parents(key, part):
    return tree_arrays(key)[0]


def draw_layout(key, part):
    return tree_arrays(key)[1]


def draw_depths(key, part):
    return tree_arrays(key)[2]


def steps_of(rng, dims, shards, least, top_value):
    level = 1.0
    for position, parts in shards:
        heights = jax.random.uniform(jax.random.fold_in(jax.random.fold_in(rng, 6), position), (parts,), jnp.float32, least / len(shards), top_value / len(shards))
        level = level * jnp.repeat(jnp.exp(heights), dims[position] // parts).reshape((-1,) + (1,) * (len(dims) - 1 - position))
    return level


def bell_draw(own_key, extent, scale, limit, cuts=(), held_as=jnp.bfloat16):
    entries = scale * jax.random.normal(own_key, extent, jnp.float32)
    if cuts:
        entries = entries * steps_of(own_key, extent, cuts, -0.22, 0.18)
    return jnp.clip(entries, -limit, limit).astype(held_as)


def setup_inputs(seed: int = 0) -> dict:
    key_of = jax.random.split(jax.random.key(seed), 17)
    inputs = bell_draw(key_of[0], (MB, TOKENS, D), 1.0, 6.0, ((1, 32),))
    depths = draw_depths(jax.random.fold_in(key_of[16], 71), 0)
    parents = draw_parents(jax.random.fold_in(key_of[16], 71), 0)
    layout = draw_layout(jax.random.fold_in(key_of[16], 71), 0)
    gain_attn = jnp.clip(1.0 + 0.1 * jax.random.normal(key_of[4], (D,), jnp.float32), 0.5, 1.5).astype(jnp.bfloat16)
    w_query = bell_draw(key_of[5], (D, QH * DH), D ** -0.5, 0.125, ((0, 8),))
    w_key = bell_draw(key_of[6], (D, KVH * DH), D ** -0.5, 0.125, ((0, 8),))
    w_value = bell_draw(key_of[7], (D, KVH * DH), D ** -0.5, 0.125, ((0, 8),))
    query_gain = jnp.clip(1.0 + 0.18 * jax.random.normal(key_of[8], (DH,), jnp.float32), 0.099609375, 1.8984375).astype(jnp.bfloat16)
    key_gain = jnp.clip(1.0 + 0.18 * jax.random.normal(key_of[9], (DH,), jnp.float32), 0.099609375, 1.8984375).astype(jnp.bfloat16)
    w_output = bell_draw(key_of[10], (QH * DH, D), (QH * DH // 64) ** -0.5, 1.0, ((0, 8),))
    gain_ffn = jnp.clip(1.0 + 0.1 * jax.random.normal(key_of[11], (D,), jnp.float32), 0.5, 1.5).astype(jnp.bfloat16)
    w_gate = bell_draw(key_of[12], (D, FF), D ** -0.5, 0.125, ((0, 8),))
    w_up = bell_draw(key_of[13], (D, FF), D ** -0.5, 0.125, ((0, 8),))
    w_down = bell_draw(key_of[14], (FF, D), FF ** -0.5, 0.078125, ((0, 8),))
    cotangent = bell_draw(key_of[15], (MB, TOKENS, D), 1.0, 6.0, ((1, 32),))
    return {"inputs": inputs, "depths": depths, "parents": parents, "layout": layout, "gain_attn": gain_attn, "w_query": w_query, "w_key": w_key, "w_value": w_value, "query_gain": query_gain, "key_gain": key_gain, "w_output": w_output, "gain_ffn": gain_ffn, "w_gate": w_gate, "w_up": w_up, "w_down": w_down, "cotangent": cotangent}


EPS = 1e-06
NEG = -1e+30
BASE = 1000000.0
HIGH = lax.Precision.HIGHEST

@jax.custom_vjp
def low(v):
    return lax.optimization_barrier(v.astype(jnp.bfloat16)).astype(jnp.float32)

@jax.custom_vjp
def low_back(v):
    return v

def low_keep(v):
    return (low(v), None)

def low_pass(kept, grad):
    return (grad,)

def back_keep(v):
    return (v, None)

def back_low(kept, grad):
    return (low(grad),)
low.defvjp(low_keep, low_pass)
low_back.defvjp(back_keep, back_low)

def rms_gain(values, gain):
    return values * lax.rsqrt(lax.optimization_barrier(jnp.mean(values * values, axis=-1, keepdims=True)) + EPS) * gain

def rotate(values, depth):
    half = values.shape[-1] // 2
    freq = jnp.power(BASE, -jnp.arange(half, dtype=jnp.float32) / half)
    angle = depth.astype(jnp.float32)[:, None] * freq[None, :]
    cosine = jnp.cos(angle)[:, None, :]
    sine = jnp.sin(angle)[:, None, :]
    first = values[..., :half]
    second = values[..., half:]
    return jnp.concatenate([first * cosine - second * sine, second * cosine + first * sine], axis=-1)

def head_post(raw, gain, depth, heads):
    shaped = raw.reshape(raw.shape[0], heads, DH)
    return rotate(rms_gain(shaped, gain), depth)

def visibility(parent, layout, offset, count):
    blocks = parent.shape[0]
    ident = jnp.arange(blocks, dtype=jnp.int32)

    def climb(step, carry):
        current, reach = carry
        current = lax.optimization_barrier(jnp.sum(jnp.where(current[:, None] == ident[None, :], parent[None, :], 0), axis=1)).astype(jnp.int32)
        return (current, reach | (current[:, None] == ident[None, :]))
    current, reach = lax.fori_loop(0, blocks, climb, (ident, ident[:, None] == ident[None, :]))
    place = (layout[:, None] == ident[None, :]).astype(jnp.int32)
    row_reach = jnp.dot(jnp.dot(place, reach.astype(jnp.int32)), place.T) > 0
    mine = lax.dynamic_slice_in_dim(row_reach, offset // BLK, count // BLK, 0)
    spread = jnp.repeat(jnp.repeat(mine, BLK, axis=0), BLK, axis=1)
    query_rows = offset + jnp.arange(count, dtype=jnp.int32)
    key_rows = jnp.arange(blocks * BLK, dtype=jnp.int32)
    same = query_rows[:, None] // BLK == key_rows[None, :] // BLK
    return spread & (jnp.logical_not(same) | (key_rows[None, :] <= query_rows[:, None]))

def matmul(left, right):
    return jnp.dot(left, right, precision=HIGH)

def layer(params, tree_in, tree_depth, tree_parent, tree_layout):
    g_attn, wq, wk, wv, gq, gk, wo, g_ffn, wg, wu, wd = params
    count = tree_in.shape[0]
    group = QH // KVH
    visible = visibility(tree_parent, tree_layout, 0, count)
    normed = low(rms_gain(tree_in, g_attn))
    query_raw = low_back(matmul(normed, wq))
    key_raw = low_back(matmul(normed, wk))
    values = low(low_back(matmul(normed, wv))).reshape(count, KVH, DH)
    queries = low(head_post(query_raw, gq, tree_depth, QH)).reshape(count, KVH, group, DH)
    keys = low(head_post(key_raw, gk, tree_depth, KVH))
    scores = low_back(jnp.einsum('qgjd,kgd->gjqk', queries, keys, precision=HIGH) * DH ** (-0.5))
    scores = jnp.where(visible[None, None], scores, NEG)
    top = lax.optimization_barrier(jnp.max(scores, axis=-1, keepdims=True))
    lse = top + jnp.log(lax.optimization_barrier(jnp.sum(jnp.exp(scores - top), axis=-1, keepdims=True)))
    weights_low = low(jnp.exp(scores - lse))
    attended = jnp.einsum('gjqk,kgd->qgjd', weights_low, values, precision=HIGH)
    attended = low(low_back(attended)).reshape(count, QH * DH)
    middle = tree_in + low_back(matmul(attended, wo))
    mid_normed = low(rms_gain(middle, g_ffn))
    gate = low_back(matmul(mid_normed, wg))
    up = low_back(matmul(mid_normed, wu))
    activated = low(jax.nn.silu(gate) * up)
    return middle + low_back(matmul(activated, wd))

def reference(inputs, depths, parents, layout, gain_attn, w_query, w_key, w_value, query_gain, key_gain, w_output, gain_ffn, w_gate, w_up, w_down, cotangent):
    trees = MB * N_FSDP
    trees_in = inputs.astype(jnp.float32).reshape(trees, TREE_TOKENS, D)
    tree_depths = depths.reshape(trees, TREE_TOKENS)
    tree_parents = parents.reshape(trees, TREE_BLOCKS)
    tree_layouts = layout.reshape(trees, TREE_BLOCKS)
    params = tuple((weight.astype(jnp.float32) for weight in (gain_attn, w_query, w_key, w_value, query_gain, key_gain, w_output, gain_ffn, w_gate, w_up, w_down)))

    def forward(params, trees_in):

        def one_tree(carry, item):
            tree_in, tree_depth, tree_parent, tree_layout = item
            return (carry, layer(params, tree_in, tree_depth, tree_parent, tree_layout))
        carry, results = lax.scan(jax.checkpoint(one_tree), jnp.float32(0.0), (trees_in, tree_depths, tree_parents, tree_layouts))
        return results
    results, backward = jax.vjp(forward, params, trees_in)
    grads, grad_in = backward(cotangent.astype(jnp.float32).reshape(trees, TREE_TOKENS, D))
    return (results.reshape(MB, TOKENS, D).astype(jnp.bfloat16), grad_in.reshape(MB, TOKENS, D), grads[0], grads[1], grads[2], grads[3], grads[4], grads[5], grads[6], grads[7], grads[8], grads[9], grads[10])
```

```python
import jax
import jax.numpy as jnp
from jax import lax
from jax.sharding import PartitionSpec as P

D = 2048
QH = 16
KVH = 8
DH = 128
FF = 6144
BLK = 128
GROUP = QH // KVH
SCALE = DH ** (-0.5)

EPS = 1e-06
NEG = -1e30
BASE = 1000000.0
BF = jnp.bfloat16
F32 = jnp.float32


def mat(left, right):
    return jnp.dot(left, right, preferred_element_type=F32)


def dot_last(left, right):
    return lax.dot_general(left, right, (((1,), (1,)), ((), ())), preferred_element_type=F32)


def outer(left, right):
    return lax.dot_general(left, right, (((0,), (0,)), ((), ())), preferred_element_type=F32)


def swap(value, bits):
    count = lax.axis_size("fsdp")
    return lax.ppermute(value, "fsdp", [(i, i ^ bits) for i in range(count)])


def inv_rms(values):
    return lax.rsqrt(jnp.mean(values * values, axis=-1, keepdims=True) + EPS)


def rms_back(values, inv, gain, dy):
    product = dy * values
    dv = inv * (gain * dy) - values * (inv * inv * inv) * jnp.mean(
        product * gain, axis=-1, keepdims=True
    )
    dg = jnp.sum(product * inv, axis=tuple(range(values.ndim - 1)))
    return dv, dg


def rotate(values, cosine, sine):
    half = values.shape[-1] // 2
    first = values[..., :half]
    second = values[..., half:]
    return jnp.concatenate(
        [first * cosine - second * sine, second * cosine + first * sine], axis=-1
    )


def visibility(parent, layout, offset, count):
    blocks = parent.shape[0]
    ident = jnp.arange(blocks, dtype=jnp.int32)
    current = ident
    reach = ident[:, None] == ident[None, :]
    for step in range(blocks):
        current = jnp.sum(jnp.where(current[:, None] == ident[None, :], parent[None, :], 0), axis=1)
        reach = reach | (current[:, None] == ident[None, :])
    place = (layout[:, None] == ident[None, :]).astype(jnp.int32)
    row_reach = jnp.dot(jnp.dot(place, reach.astype(jnp.int32)), place.T) > 0
    mine = lax.dynamic_slice_in_dim(row_reach, offset // BLK, count // BLK, 0)
    spread = jnp.repeat(jnp.repeat(mine, BLK, axis=0), BLK, axis=1)
    query_rows = offset + jnp.arange(count, dtype=jnp.int32)
    key_rows = jnp.arange(blocks * BLK, dtype=jnp.int32)
    same = query_rows[:, None] // BLK == key_rows[None, :] // BLK
    return spread & (jnp.logical_not(same) | (key_rows[None, :] <= query_rows[:, None]))


def gather_small(vector, me):
    count = lax.axis_size("fsdp")
    buffer = jnp.zeros((count,) + vector.shape, vector.dtype)
    buffer = lax.dynamic_update_index_in_dim(buffer, vector, me, 0)
    step = 1
    while step < count:
        buffer = buffer + swap(buffer, step)
        step *= 2
    return buffer


def gather_columns(shard, me):
    count = lax.axis_size("fsdp")
    high = count // 4
    slot = me % 4
    mine_high = me // 4
    rows = shard.shape[0]
    unit = shard.shape[1] // count
    split = shard.reshape(rows, high, 4, unit)

    def part(which):
        return lax.dynamic_index_in_dim(split, which, axis=2, keepdims=False).reshape(
            rows, high * unit
        )

    own = part(slot)
    from_x_mate = swap(part(slot ^ 3), 2)
    from_x = swap(part(slot ^ 2), 2)
    from_core = swap(part(slot ^ 1), 1)
    from_both = swap(from_x_mate, 1)
    pieces = [own, from_core, from_x, from_both]
    buffer = jnp.zeros((count * rows, high * unit), shard.dtype)
    for far in range(high):
        for near in range(4):
            piece = pieces[near] if far == 0 else swap(pieces[near], 4 * far)
            place = (mine_high ^ far) * 4 + (slot ^ near)
            buffer = lax.dynamic_update_slice_in_dim(buffer, piece, place * rows, 0)
    return buffer


def gather_rows(shard, me):
    count = lax.axis_size("fsdp")
    high = count // 4
    mine_high = me // 4
    unit = shard.shape[0]
    buffer = jnp.zeros((high * unit, shard.shape[1]), shard.dtype)
    for far in range(high):
        piece = shard if far == 0 else swap(shard, 4 * far)
        buffer = lax.dynamic_update_slice_in_dim(buffer, piece, (mine_high ^ far) * unit, 0)
    return buffer


def group_rows(rows):
    from_x = swap(rows, 2)
    from_core = swap(rows, 1)
    from_both = swap(from_x, 1)
    return jnp.concatenate([rows, from_core, from_x, from_both], axis=0)


def group_sum(partial):
    rows = partial.shape[0] // 4
    part = [partial[i * rows : (i + 1) * rows] for i in range(4)]
    for_x = part[2] + swap(part[3].astype(BF), 1).astype(F32)
    got_x = swap(for_x.astype(BF), 2)
    got_core = swap(part[1].astype(BF), 1)
    return part[0] + got_core.astype(F32) + got_x.astype(F32)


def sum_high(gradient, me):
    count = lax.axis_size("fsdp")
    high = count // 4
    mine_high = me // 4
    rows = gradient.shape[0] // high

    def part(which):
        return lax.dynamic_slice_in_dim(gradient, which * rows, rows, 0)

    total = None
    for far in range(1, high):
        got = swap(part(mine_high ^ far).astype(BF), 4 * far).astype(F32)
        total = got if total is None else total + got
    own = part(mine_high)
    return (own if total is None else own + total).astype(BF)


def spread_columns(gradient, me):
    count = lax.axis_size("fsdp")
    high = count // 4
    depth = lax.axis_size("ctx")
    slot = me % 4
    summed = sum_high(gradient, me)
    rows = summed.shape[0] // 4
    cols = summed.shape[1]
    unit = cols // high
    chunks = jnp.swapaxes(summed.reshape(4, depth, rows // depth, cols), 0, 1)
    piece = lax.psum_scatter(
        chunks.reshape(4 * rows, cols), "ctx", scatter_dimension=0, tiled=True
    ).reshape(4, rows // depth, cols)

    def part(which):
        return lax.dynamic_index_in_dim(piece, which, axis=0, keepdims=False)

    result = jnp.zeros((rows // depth, high, 4, unit), BF)
    for near in range(4):
        got = part(slot ^ near)
        if near:
            got = swap(got, near)
        result = lax.dynamic_update_slice(
            result, got.reshape(rows // depth, high, 1, unit), (0, 0, slot ^ near, 0)
        )
    result = result.reshape(rows // depth, count * unit)
    return lax.all_gather(result, "ctx", axis=0, tiled=True)


def spread_rows(gradient, me):
    summed = sum_high(gradient, me)
    piece = lax.psum_scatter(summed, "ctx", scatter_dimension=0, tiled=True)
    return lax.all_gather(piece, "ctx", axis=0, tiled=True)


def scatter_plain(gradient):
    piece = lax.psum_scatter(gradient.astype(BF), "fsdp", scatter_dimension=0, tiled=True)
    return lax.psum(piece, "ctx")


def scores_of(queries, keys_all, visible):
    scores = (
        jnp.einsum("qgjd,kgd->gjqk", queries, keys_all, preferred_element_type=F32) * SCALE
    )
    return jnp.where(visible[None, None], scores, NEG)


def body(
    inputs,
    depths,
    parents,
    layout,
    gain_attn,
    w_query,
    w_key,
    w_value,
    query_gain,
    key_gain,
    w_output,
    gain_ffn,
    w_gate,
    w_up,
    w_down,
    cotangent,
):
    me = lax.axis_index("fsdp")
    micro, local, _ = inputs.shape
    total = micro * local
    blocks = parents.shape[2]
    tree_rows = blocks * BLK
    offset = lax.axis_index("ctx") * local
    count = lax.axis_size("fsdp")

    w_qkv = lax.all_gather(
        jnp.concatenate([w_query, w_key, w_value], axis=1), "fsdp", axis=0, tiled=True
    )
    w_out = lax.all_gather(w_output, "fsdp", axis=0, tiled=True)
    gains = gather_small(jnp.concatenate([gain_attn, gain_ffn, query_gain, key_gain]), me)
    shard = D // count
    head_shard = DH // count
    attn_gain = gains[:, :shard].reshape(D).astype(F32)
    ffn_gain = gains[:, shard : 2 * shard].reshape(D).astype(F32)
    q_gain = gains[:, 2 * shard : 2 * shard + head_shard].reshape(DH).astype(F32)
    k_gain = gains[:, 2 * shard + head_shard :].reshape(DH).astype(F32)

    cot_b = cotangent.reshape(total, D)
    wd = gather_rows(w_down, me)
    wg = gather_columns(w_gate, me)
    wu = gather_columns(w_up, me)
    cot_rows = group_rows(cot_b)

    source = inputs.reshape(total, D).astype(F32)
    inv_in = inv_rms(source)
    normed_b = (source * inv_in * attn_gain).astype(BF)
    raw = mat(normed_b, w_qkv)
    query_raw = raw[:, : QH * DH].reshape(total, QH, DH)
    key_raw = raw[:, QH * DH : (QH + KVH) * DH].reshape(total, KVH, DH)
    value_b = raw[:, (QH + KVH) * DH :].astype(BF)
    freq = jnp.power(BASE, -jnp.arange(DH // 2, dtype=F32) / (DH // 2))
    angle = depths.reshape(total).astype(F32)[:, None] * freq[None, :]
    cosine = jnp.cos(angle)[:, None, :]
    sine = jnp.sin(angle)[:, None, :]
    inv_q = inv_rms(query_raw)
    inv_k = inv_rms(key_raw)
    key_b = rotate(key_raw * inv_k * k_gain, cosine, sine).astype(BF).reshape(total, KVH * DH)
    queries = rotate(query_raw * inv_q * q_gain, cosine, sine).astype(BF)

    attended = []
    saved = []
    for index in range(micro):
        part = slice(index * local, (index + 1) * local)
        visible = visibility(parents[index, 0], layout[index, 0], offset, local)
        both = lax.all_gather(
            jnp.concatenate([key_b[part], value_b[part]], axis=1), "ctx", axis=0, tiled=True
        )
        keys_all = both[:, : KVH * DH].reshape(tree_rows, KVH, DH)
        values_all = both[:, KVH * DH :].reshape(tree_rows, KVH, DH)
        query_part = queries[part].reshape(local, KVH, GROUP, DH)
        scores = scores_of(query_part, keys_all, visible)
        top = jnp.max(scores, axis=-1, keepdims=True)
        lse = top + jnp.log(jnp.sum(jnp.exp(scores - top), axis=-1, keepdims=True))
        probs_low = jnp.exp(scores - lse).astype(BF)
        out = jnp.einsum("gjqk,kgd->qgjd", probs_low, values_all, preferred_element_type=F32)
        attended.append(out.reshape(local, QH * DH).astype(BF))
        saved.append((query_part, keys_all, values_all, visible, lse))
    attended_b = jnp.concatenate(attended, axis=0)

    middle = source + mat(attended_b, w_out)
    inv_mid = inv_rms(middle)
    mid_b = (middle * inv_mid * ffn_gain).astype(BF)
    mid_rows = group_rows(mid_b)
    d_act = dot_last(cot_rows, wd)
    gate = mat(mid_rows, wg)
    up = mat(mid_rows, wu)
    sig = jax.nn.sigmoid(gate)
    silu = gate * sig
    act_b = (silu * up).astype(BF)
    dup_b = (d_act * silu).astype(BF)
    dgate_b = (d_act * up * (sig * (1.0 + gate * (1.0 - sig)))).astype(BF)
    outputs = (middle + group_sum(mat(act_b, wd))).astype(BF)
    d_mid = group_sum(dot_last(dgate_b, wg) + dot_last(dup_b, wu))
    grad_down = spread_rows(outer(act_b, cot_rows), me)
    grad_gate = spread_columns(outer(mid_rows, dgate_b), me)
    grad_up = spread_columns(outer(mid_rows, dup_b), me)

    d_part, d_ffn_gain = rms_back(middle, inv_mid, ffn_gain, d_mid)
    d_middle = cot_b.astype(F32) + d_part
    dproj_b = d_middle.astype(BF)
    d_attended = dot_last(dproj_b, w_out).astype(BF)
    grad_output = scatter_plain(outer(attended_b, dproj_b))

    d_query_parts = []
    d_kv_parts = []
    for index in range(micro):
        part = slice(index * local, (index + 1) * local)
        query_part, keys_all, values_all, visible, lse = saved[index]
        d_out = d_attended[part].reshape(local, KVH, GROUP, DH)
        probs = jnp.exp(scores_of(query_part, keys_all, visible) - lse)
        probs_low = probs.astype(BF)
        d_probs = jnp.einsum("qgjd,kgd->gjqk", d_out, values_all, preferred_element_type=F32)
        d_scores = (probs * (d_probs - jnp.sum(probs * d_probs, axis=-1, keepdims=True))).astype(BF)
        d_query = (
            jnp.einsum("gjqk,kgd->qgjd", d_scores, keys_all, preferred_element_type=F32) * SCALE
        )
        d_key = (
            jnp.einsum("gjqk,qgjd->kgd", d_scores, query_part, preferred_element_type=F32) * SCALE
        )
        d_value = jnp.einsum("gjqk,qgjd->kgd", probs_low, d_out, preferred_element_type=F32)
        d_query_parts.append(d_query.reshape(local, QH, DH))
        d_kv_parts.append(
            lax.psum_scatter(
                jnp.concatenate(
                    [
                        d_key.reshape(tree_rows, KVH * DH).astype(BF),
                        d_value.reshape(tree_rows, KVH * DH).astype(BF),
                    ],
                    axis=1,
                ),
                "ctx",
                scatter_dimension=0,
                tiled=True,
            )
        )
    d_queries = jnp.concatenate(d_query_parts, axis=0)
    d_kv = jnp.concatenate(d_kv_parts, axis=0)
    d_keys = d_kv[:, : KVH * DH].astype(F32).reshape(total, KVH, DH)
    dvalue_b = d_kv[:, KVH * DH :]
    dquery_raw, d_q_gain = rms_back(query_raw, inv_q, q_gain, rotate(d_queries, cosine, -sine))
    dkey_raw, d_k_gain = rms_back(key_raw, inv_k, k_gain, rotate(d_keys, cosine, -sine))
    d_q_gain = d_q_gain
    dqkv_b = jnp.concatenate(
        [
            dquery_raw.astype(BF).reshape(total, QH * DH),
            dkey_raw.astype(BF).reshape(total, KVH * DH),
            dvalue_b,
        ],
        axis=1,
    )
    grad_qkv = scatter_plain(outer(normed_b, dqkv_b))
    d_normed = dot_last(dqkv_b, w_qkv)
    d_source, d_attn_gain = rms_back(source, inv_in, attn_gain, d_normed)
    grad_inputs = (d_middle + d_source).reshape(micro, local, D)

    sums = lax.psum(
        jnp.concatenate([d_attn_gain, d_ffn_gain, d_q_gain, d_k_gain]), ("fsdp", "ctx")
    )

    def own(vector):
        size = vector.shape[0] // count
        return lax.dynamic_slice_in_dim(vector, me * size, size, 0)

    return (
        outputs.reshape(micro, local, D),
        grad_inputs,
        own(sums[:D]),
        grad_qkv[:, : QH * DH].astype(F32),
        grad_qkv[:, QH * DH : (QH + KVH) * DH].astype(F32),
        grad_qkv[:, (QH + KVH) * DH :].astype(F32),
        own(sums[2 * D : 2 * D + DH]),
        own(sums[2 * D + DH :]),
        grad_output.astype(F32),
        own(sums[D : 2 * D]),
        grad_gate.astype(F32),
        grad_up.astype(F32),
        grad_down.astype(F32),
    )


def solution(mesh):
    rows = P(None, ("fsdp", "ctx"), None)
    tree = P(None, "fsdp", None)
    vector = P("fsdp")
    weight = P("fsdp", None)
    in_specs = (
        rows,
        P(None, ("fsdp", "ctx")),
        tree,
        tree,
        vector,
        weight,
        weight,
        weight,
        vector,
        vector,
        weight,
        vector,
        weight,
        weight,
        weight,
        rows,
    )
    out_specs = (
        rows,
        rows,
        vector,
        weight,
        weight,
        weight,
        vector,
        vector,
        weight,
        vector,
        weight,
        weight,
        weight,
    )
    return jax.shard_map(body, mesh=mesh, in_specs=in_specs, out_specs=out_specs, check_vma=False)
```

```python
import functools

import jax
import jax.numpy as jnp
from jax import lax
from jax.experimental import pallas as pl
from jax.experimental.pallas import tpu as pltpu
from jax.sharding import PartitionSpec as P

D = 2048
QH = 16
KVH = 8
DH = 128
FF = 6144
BLK = 128
GROUP = QH // KVH
SCALE = DH ** (-0.5)
LOG2E = 1.4426950408889634

EPS = 1e-06
BASE = 1000000.0
BF = jnp.bfloat16
F32 = jnp.float32
BLOCK = 512
COST = 100.0
LOW = 0.01
VMEM = 60 * 1024 * 1024


def mat(left, right):
    return jnp.dot(left, right, preferred_element_type=F32)


def dot_last(left, right):
    return lax.dot_general(left, right, (((1,), (1,)), ((), ())), preferred_element_type=F32)


def outer(left, right):
    return lax.dot_general(left, right, (((0,), (0,)), ((), ())), preferred_element_type=F32)


def after(value, *others):
    return lax.optimization_barrier((value,) + others)[0]


def swap(value, bits):
    count = lax.axis_size("fsdp")
    return lax.ppermute(value, "fsdp", [(i, i ^ bits) for i in range(count)])


def inv_rms(values):
    return lax.rsqrt(jnp.mean(values * values, axis=-1, keepdims=True) + EPS)


def rms_back(values, inv, gain, dy):
    product = dy * values
    dv = inv * (gain * dy) - values * (inv * inv * inv) * jnp.mean(
        product * gain, axis=-1, keepdims=True
    )
    return dv, jnp.sum(product * inv, axis=0)


def call(
    kernel,
    name,
    grid,
    in_specs,
    out_specs,
    out_shape,
    flops,
    moved,
    scratch=(),
    aliases=None,
    scalars=0,
    cost=COST,
):
    return pl.pallas_call(
        kernel,
        name=name,
        grid_spec=pltpu.PrefetchScalarGridSpec(
            num_scalar_prefetch=scalars,
            grid=grid,
            in_specs=in_specs,
            out_specs=out_specs,
            scratch_shapes=list(scratch),
        ),
        out_shape=out_shape,
        input_output_aliases=aliases or {},
        compiler_params=pltpu.CompilerParams(vmem_limit_bytes=VMEM),
        cost_estimate=pl.CostEstimate(
            flops=int(flops * cost), bytes_accessed=int(moved * cost), transcendentals=0
        ),
    )


def fixed(shape):
    return pl.BlockSpec(
        shape, lambda *index: tuple(0 for _ in shape), pipeline_mode=pl.Buffered(1)
    )


def project(x, weight, first, cols, cosine, sine, gain, kinds, name):
    rows, depth = x.shape
    width = DH * len(kinds)

    def kernel(x_ref, w_ref, c_ref, s_ref, g_ref, out_ref, raw_ref):
        raw = mat(x_ref[...], w_ref[...])
        raw_ref[...] = raw.astype(BF)
        for index, kind in enumerate(kinds):
            part = raw[:, index * DH : (index + 1) * DH]
            if kind == "r":
                part = part * inv_rms(part) * g_ref[...]
                part = part * c_ref[...] + pltpu.roll(part, DH // 2, 1) * s_ref[...]
            out_ref[:, index * DH : (index + 1) * DH] = part.astype(BF)

    whole = lambda j: (0, 0)
    block = lambda j: (0, j)
    return call(
        kernel,
        name,
        (cols // width,),
        [
            pl.BlockSpec((rows, depth), whole),
            pl.BlockSpec((depth, width), lambda j: (0, j + first // width)),
            pl.BlockSpec((rows, DH), whole),
            pl.BlockSpec((rows, DH), whole),
            pl.BlockSpec((1, DH), whole),
        ],
        [pl.BlockSpec((rows, width), block)] * 2,
        [jax.ShapeDtypeStruct((rows, cols), BF)] * 2,
        2 * rows * depth * cols,
        2 * (rows * depth + depth * cols + 2 * rows * cols),
    )(x, weight, cosine, sine, gain)


def stack_heads(block):
    return jnp.concatenate([block[:, i * DH : (i + 1) * DH] for i in range(GROUP)], axis=0)


def attention(queries, pairs, mask):
    rows = queries.shape[0]
    keys = pairs.shape[0]

    def kernel(q_ref, kv_ref, m_ref, out_ref, inv_ref):
        stacked = stack_heads(q_ref[...])
        scores = dot_last(kv_ref[:, :DH], stacked)
        mask_now = jnp.concatenate([m_ref[...]] * GROUP, axis=1)
        powers = jnp.exp2(scores * (SCALE * LOG2E)) * mask_now
        inv = 1.0 / jnp.sum(powers, axis=0, keepdims=True)
        inv_ref[0] = inv
        out = (outer(kv_ref[:, DH:], powers.astype(BF)) * inv).T
        for index in range(GROUP):
            out_ref[:, index * DH : (index + 1) * DH] = out[
                index * rows : (index + 1) * rows
            ].astype(BF)

    return call(
        kernel,
        "attention",
        (KVH,),
        [
            pl.BlockSpec((rows, GROUP * DH), lambda g: (0, g)),
            pl.BlockSpec((keys, 2 * DH), lambda g: (0, g)),
            pl.BlockSpec((keys, rows), lambda g: (0, 0)),
        ],
        [
            pl.BlockSpec((rows, GROUP * DH), lambda g: (0, g)),
            pl.BlockSpec((1, 1, GROUP * rows), lambda g: (g, 0, 0)),
        ],
        [
            jax.ShapeDtypeStruct((rows, QH * DH), BF),
            jax.ShapeDtypeStruct((KVH, 1, GROUP * rows), F32),
        ],
        4 * QH * rows * keys * DH,
        2 * (2 * rows * QH * DH + 2 * keys * KVH * DH),
    )(queries, pairs, mask)


def head_back(dy, raw, cosine, sine, gain):
    turned = dy * cosine - pltpu.roll(dy, DH // 2, 1) * sine
    inv = inv_rms(raw)
    product = turned * raw
    dv = inv * (gain * turned) - raw * (inv * inv * inv) * jnp.mean(
        product * gain, axis=-1, keepdims=True
    )
    return dv, jnp.sum(product * inv, axis=0, keepdims=True)


def attention_back(queries, raw, pairs, mask, d_out, out, inv, cosine, sine, gain):
    rows = queries.shape[0]
    keys = pairs.shape[0]

    def kernel(
        q_ref, r_ref, kv_ref, m_ref, do_ref, o_ref, inv_ref, c_ref, s_ref, g_ref,
        dq_ref, dkv_ref, dg_ref,
    ):
        stacked = stack_heads(q_ref[...])
        d_stacked = stack_heads(do_ref[...])
        o_stacked = stack_heads(o_ref[...])
        dots = jnp.sum((d_stacked.astype(F32) * o_stacked.astype(F32)).T, axis=0, keepdims=True)
        scores = dot_last(kv_ref[:, :DH], stacked)
        mask_now = jnp.concatenate([m_ref[...]] * GROUP, axis=1)
        probs = jnp.exp2(scores * (SCALE * LOG2E)) * (mask_now * inv_ref[0])
        d_probs = dot_last(kv_ref[:, DH:], d_stacked)
        d_scores = (probs * (d_probs - dots)).astype(BF)
        dkv_ref[:, DH:] = mat(probs.astype(BF), d_stacked).astype(BF)
        dkv_ref[:, :DH] = (mat(d_scores, stacked) * SCALE).astype(BF)
        d_query = outer(d_scores, kv_ref[:, :DH]) * SCALE
        total = jnp.zeros((1, DH), F32)
        for index in range(GROUP):
            part = slice(index * DH, (index + 1) * DH)
            dv, dg = head_back(
                d_query[index * rows : (index + 1) * rows],
                r_ref[:, part].astype(F32),
                c_ref[...],
                s_ref[...],
                g_ref[...],
            )
            dq_ref[:, part] = dv.astype(BF)
            total = total + dg

        @pl.when(pl.program_id(0) == 0)
        def _():
            dg_ref[...] = jnp.zeros_like(dg_ref)

        dg_ref[...] += total

    head = pl.BlockSpec((rows, GROUP * DH), lambda g: (0, g))
    pair = pl.BlockSpec((keys, 2 * DH), lambda g: (0, g))
    whole = lambda shape: pl.BlockSpec(shape, lambda g: (0, 0))
    return call(
        kernel,
        "attention_back",
        (KVH,),
        [
            head,
            head,
            pair,
            whole((keys, rows)),
            head,
            head,
            pl.BlockSpec((1, 1, GROUP * rows), lambda g: (g, 0, 0)),
            whole((rows, DH)),
            whole((rows, DH)),
            whole((1, DH)),
        ],
        [head, pair, whole((1, DH))],
        [
            jax.ShapeDtypeStruct((rows, QH * DH), BF),
            jax.ShapeDtypeStruct((keys, 2 * KVH * DH), BF),
            jax.ShapeDtypeStruct((1, DH), F32),
        ],
        10 * QH * rows * keys * DH,
        2 * (5 * rows * QH * DH + 4 * keys * KVH * DH),
    )(queries, raw, pairs, mask, d_out, out, inv, cosine, sine, gain)


def pair_back(d_pairs, raw, cosine, sine, gain):
    rows, cols = d_pairs.shape

    def kernel(d_ref, r_ref, c_ref, s_ref, g_ref, out_ref, dg_ref):
        total = jnp.zeros((1, DH), F32)
        for index in range(BLOCK // (2 * DH)):
            part = slice(index * 2 * DH, index * 2 * DH + DH)
            rest = slice(index * 2 * DH + DH, (index + 1) * 2 * DH)
            dv, dg = head_back(
                d_ref[:, part].astype(F32),
                r_ref[:, part].astype(F32),
                c_ref[...],
                s_ref[...],
                g_ref[...],
            )
            out_ref[:, part] = dv.astype(BF)
            out_ref[:, rest] = d_ref[:, rest]
            total = total + dg

        @pl.when(pl.program_id(0) == 0)
        def _():
            dg_ref[...] = jnp.zeros_like(dg_ref)

        dg_ref[...] += total

    block = pl.BlockSpec((rows, BLOCK), lambda j: (0, j))
    whole = lambda shape: pl.BlockSpec(shape, lambda j: (0, 0))
    return call(
        kernel,
        "pair_back",
        (cols // BLOCK,),
        [block, block, whole((rows, DH)), whole((rows, DH)), whole((1, DH))],
        [block, whole((1, DH))],
        [jax.ShapeDtypeStruct((rows, cols), BF), jax.ShapeDtypeStruct((1, DH), F32)],
        20 * rows * cols,
        6 * rows * cols,
        cost=LOW,
    )(d_pairs, raw, cosine, sine, gain)


def feed(mids, cots, pieces, w_down, index, total, earlier, place):
    rows, depth = mids[0].shape
    parts = len(mids)
    hidden = w_down.shape[0]
    count = len(pieces)
    unit = place[1]
    steps = hidden // unit
    block_rows = depth // (4 * count)

    def kernel(me_ref, *refs):
        mid_refs = refs[:parts]
        cot_refs = refs[parts : 2 * parts]
        piece_refs = refs[2 * parts : 2 * parts + count]
        wd_ref = refs[2 * parts + count]
        if count > 1:
            act_ref, d_ref, wp_ref = refs[-3:]
            for which in range(4 * count):
                start = pl.multiple_of((me_ref[0] ^ which) * block_rows, block_rows)
                near = which % 4 * block_rows
                wp_ref[pl.ds(start, block_rows), :] = piece_refs[which // 4][
                    near : near + block_rows
                ]
        else:
            act_ref, d_ref = refs[-2:]
            wp_ref = piece_refs[0]
        for part in range(parts):
            now = slice(part * rows, (part + 1) * rows)
            both = mat(mid_refs[part][...], wp_ref[...])
            gate = both[:, :unit]
            up = both[:, unit:]
            d_act = dot_last(cot_refs[part][...], wd_ref[...])
            sig = 1.0 / (1.0 + jnp.exp2(gate * (-LOG2E)))
            silu = gate * sig
            act_ref[now] = (silu * up).astype(BF)
            d_ref[now, unit:] = (d_act * silu).astype(BF)
            d_ref[now, :unit] = (d_act * up * (sig + silu * (1.0 - sig))).astype(BF)

    def piece_spec(far):
        return pl.BlockSpec((pieces[0].shape[0], 2 * unit), lambda j, me: (0, j ^ far))

    out_specs = [
        pl.BlockSpec((parts * rows, unit), lambda j, me: (index, j)),
        pl.BlockSpec((parts * rows, 2 * unit), lambda j, me: (index, j)),
    ]
    out_shape = [
        jax.ShapeDtypeStruct((total * parts * rows, hidden), BF),
        jax.ShapeDtypeStruct((total * parts * rows, 2 * hidden), BF),
    ]
    if count > 1:
        out_specs.append(pl.BlockSpec((depth, 2 * unit), lambda j, me: (0, j)))
        out_shape.append(jax.ShapeDtypeStruct((depth, 2 * hidden), BF))
    before = 1 + 2 * parts + count + 1
    return call(
        kernel,
        "feed",
        (steps,),
        [fixed((rows, depth))] * parts
        + [
            pl.BlockSpec(
                (rows, depth), lambda j, me: (index, 0), pipeline_mode=pl.Buffered(1)
            )
        ]
        * parts
        + [piece_spec(which) for which in range(count)]
        + [pl.BlockSpec((unit, depth), lambda j, me: (j, 0))]
        + [pl.BlockSpec(memory_space=pl.ANY)] * len(earlier),
        out_specs,
        out_shape,
        6 * parts * rows * depth * hidden,
        2 * (2 * parts * rows * depth + 3 * depth * hidden + 3 * parts * rows * hidden),
        aliases={before + i: i for i in range(len(earlier))},
        scalars=1,
    )(place[0], *mids, *cots, *pieces, w_down, *earlier)


def feed_out(left, weight, index, parts, transposed, name):
    depth = left.shape[1]
    cols = weight.shape[0] if transposed else weight.shape[1]
    rows = parts[1]

    def kernel(a_ref, w_ref, *outs):
        for part in range(parts[0]):
            now = a_ref[part * rows : (part + 1) * rows]
            result = dot_last(now, w_ref[...]) if transposed else mat(now, w_ref[...])
            outs[part][...] = result.astype(BF)

    return call(
        kernel,
        name,
        (cols // BLOCK,),
        [
            pl.BlockSpec((parts[0] * rows, depth), lambda j: (index, 0)),
            pl.BlockSpec((BLOCK, depth), lambda j: (j, 0))
            if transposed
            else pl.BlockSpec((depth, BLOCK), lambda j: (0, j)),
        ],
        [pl.BlockSpec((rows, BLOCK), lambda j: (0, j))] * parts[0],
        [jax.ShapeDtypeStruct((rows, cols), BF)] * parts[0],
        2 * parts[0] * rows * depth * cols,
        2 * (parts[0] * rows * (depth + cols) + depth * cols),
    )(left, weight)


def weight_terms(lefts, block, starts, width, size, rights, step, added, chunked, name, turn=0, cost=COST):
    depth = sum(left.shape[0] for left in lefts)
    cols = rights[0][0].shape[1]
    size_right = depth // len(rights)
    blocks = starts.shape[0]
    rows = blocks * size
    steps = cols // step
    nl, nr = len(lefts), len(rights)

    def kernel(block_ref, start_ref, *refs):
        left_refs = refs[:nl]
        right_refs = refs[nl : nl + nr]
        add_refs = refs[nl + nr : nl + nr + len(added)]
        out_ref, turned = refs[-2:]

        @pl.when(pl.program_id(0) == 0)
        def _():
            for which in range(blocks):
                start = pl.multiple_of(start_ref[which], 128)
                at = 0
                for ref in left_refs:
                    turned[which * size : (which + 1) * size, at : at + ref.shape[0]] = ref[
                        :, pl.ds(start, size)
                    ].T
                    at += ref.shape[0]

        right = [ref[...] for ref in right_refs]
        right = right[0] if nr == 1 else jnp.concatenate(right, axis=0)
        result = mat(turned[...], right)
        for ref in add_refs:
            result = result + ref[...].astype(F32)
        out_ref[...] = result.astype(BF)

    if chunked:
        out_spec = pl.BlockSpec((rows, step), lambda j, b, s: (j ^ turn, 0))
        shape = (steps * rows, step)
    else:
        out_spec = pl.BlockSpec((rows, step), lambda j, b, s: (0, j))
        shape = (rows, cols)
    return call(
        kernel,
        name,
        (steps,),
        [
            pl.BlockSpec(
                (left.shape[0], width), lambda j, b, s: (0, b[0]), pipeline_mode=pl.Buffered(1)
            )
            for left in lefts
        ]
        + [
            pl.BlockSpec((size_right, step), functools.partial(lambda at, j, b, s: (at, j), at))
            for right, at in rights
        ]
        + [out_spec] * len(added),
        out_spec,
        jax.ShapeDtypeStruct(shape, BF),
        2 * rows * depth * cols,
        2 * (rows * depth + depth * cols + (1 + len(added)) * rows * cols),
        scratch=[pltpu.VMEM((rows, depth), BF)],
        scalars=2,
        cost=cost,
    )(block, starts, *lefts, *[right for right, at in rights], *added)


def column_parts(gate, up, high, slots, number):
    rows, cols = gate.shape
    unit = cols // (4 * high)

    def kernel(slot_ref, gate_ref, up_ref, out_ref):
        out_ref[:, :unit] = gate_ref[...]
        out_ref[:, unit:] = up_ref[...]

    block = pl.BlockSpec((rows, unit), lambda i, j, at: (0, (at[0] ^ j) * 4 + at[i + 1]))
    return call(
        kernel,
        "column_parts",
        (number, high),
        [block, block],
        pl.BlockSpec((rows, 2 * unit), lambda i, j, at: (i, j)),
        jax.ShapeDtypeStruct((number * rows, 2 * unit * high), BF),
        0,
        8 * number * rows * unit * high,
        scalars=1,
    )(slots, gate, up)


def lay_pairs(chunks, place, high, unit):
    depth = len(chunks)
    rows = chunks[0].shape[1]
    cols = 4 * high * unit
    size = rows // 4

    def kernel(place_ref, *refs):
        gate_ref, up_ref = refs[-2:]
        for which in range(depth):
            chunk = place_ref[0] ^ which
            far = place_ref[1] ^ (chunk // 2)
            for near in range(4):
                start = pl.multiple_of((far * 4 + (place_ref[2] ^ near)) * unit, 128)

                @pl.when(chunk % 2 == 0)
                def _():
                    gate_ref[:, pl.ds(start, unit)] = refs[which][near].astype(F32)

                @pl.when(chunk % 2 == 1)
                def _():
                    up_ref[:, pl.ds(start, unit)] = refs[which][near].astype(F32)

    return call(
        kernel,
        "lay_pairs",
        (4,),
        [pl.BlockSpec((4, size, unit), lambda i, at: (0, i, 0))] * depth,
        [pl.BlockSpec((size, cols), lambda i, at: (i, 0))] * 2,
        [jax.ShapeDtypeStruct((rows, cols), F32)] * 2,
        0,
        12 * rows * cols,
        scalars=1,
    )(place, *chunks)


def visibility(parent, layout, offset, count):
    blocks = parent.shape[0]
    ident = jnp.arange(blocks, dtype=jnp.int32)
    current = ident
    reach = ident[:, None] == ident[None, :]
    for step in range(blocks):
        current = jnp.sum(jnp.where(current[:, None] == ident[None, :], parent[None, :], 0), axis=1)
        reach = reach | (current[:, None] == ident[None, :])
    place = (layout[:, None] == ident[None, :]).astype(jnp.int32)
    picked = jnp.sum(place[:, :, None] * reach.astype(jnp.int32)[None, :, :], axis=1)
    row_reach = jnp.sum(picked[:, None, :] * place[None, :, :], axis=2) > 0
    mine = lax.dynamic_slice_in_dim(row_reach, offset // BLK, count // BLK, 0).T
    spread = jnp.broadcast_to(
        mine[:, None, :, None], (blocks, BLK, count // BLK, BLK)
    ).reshape(blocks * BLK, count)
    query_rows = offset + lax.broadcasted_iota(jnp.int32, (blocks * BLK, count), 1)
    key_rows = lax.broadcasted_iota(jnp.int32, (blocks * BLK, count), 0)
    same = query_rows // BLK == key_rows // BLK
    return (spread & (jnp.logical_not(same) | (key_rows <= query_rows))).astype(F32)


def gather_small(vector, me):
    count = lax.axis_size("fsdp")
    buffer = jnp.zeros((count,) + vector.shape, vector.dtype)
    buffer = lax.dynamic_update_index_in_dim(buffer, vector, me, 0)
    step = 1
    while step < count:
        buffer = buffer + swap(buffer, step)
        step *= 2
    return buffer


def gather_rows(shard):
    high = lax.axis_size("fsdp") // 4
    return jnp.concatenate(
        [shard] + [swap(shard, 4 * far) for far in range(1, high)], axis=0
    )


def group_rows(rows):
    from_x = swap(rows, 2)
    from_core = swap(rows, 1)
    from_both = swap(from_x, 1)
    return [rows, from_core, from_x, from_both]


def group_sum(parts):
    for_x = (parts[2].astype(F32) + swap(parts[3], 1).astype(F32)).astype(BF)
    got_x = swap(for_x, 2)
    got_core = swap(parts[1], 1)
    return parts[0].astype(F32) + got_core.astype(F32) + got_x.astype(F32)


def group_half(parts):
    got = swap(jnp.concatenate([parts[1], parts[3]], axis=0), 1)
    rows = parts[0].shape[0]
    own = parts[0].astype(F32) + got[:rows].astype(F32)
    return own, (parts[2].astype(F32) + got[rows:].astype(F32)).astype(BF)


def gather_ctx(chunk):
    count = lax.axis_size("ctx")
    return [chunk] + [
        lax.ppermute(chunk, "ctx", [(i, i ^ step) for i in range(count)])
        for step in range(1, count)
    ]


def scatter_ctx(array):
    return lax.psum_scatter(array, "ctx", scatter_dimension=0, tiled=True)


def spread_pairs(piece, me, unit):
    high = lax.axis_size("fsdp") // 4
    slot = me % 4
    rows = piece.shape[0] // 4
    near = [lax.dynamic_slice_in_dim(piece, (slot ^ which) * rows, rows, 0) for which in range(4)]
    near = [near[0]] + [swap(near[which], which) for which in range(1, 4)]
    chunks = gather_ctx(jnp.stack(near))
    place = jnp.stack([lax.axis_index("ctx"), me // 4, slot])
    return lay_pairs(chunks, place, high, unit)


def fold(value, bits, *others):
    for bit in bits:
        half = value.shape[0] // 2
        got = swap(value[half:], bit)
        keep = after(value[:half], *others) if others else value[:half]
        value = (keep.astype(F32) + got.astype(F32)).astype(BF)
        others = ()
    return value


def order_of(bits):
    order = [0]
    for bit in reversed(bits):
        order = order + [entry ^ bit for entry in order]
    return order


def body(
    inputs,
    depths,
    parents,
    layout,
    gain_attn,
    w_query,
    w_key,
    w_value,
    query_gain,
    key_gain,
    w_output,
    gain_ffn,
    w_gate,
    w_up,
    w_down,
    cotangent,
):
    me = lax.axis_index("fsdp")
    micro, local, _ = inputs.shape
    total = micro * local
    offset = lax.axis_index("ctx") * local
    count = lax.axis_size("fsdp")
    shard = D // count
    head_shard = DH // count

    def rows_of(index):
        return slice(index * local, (index + 1) * local)

    pair_shard = jnp.stack(
        [w_key.reshape(shard, KVH, DH), w_value.reshape(shard, KVH, DH)], axis=2
    ).reshape(shard, 2 * KVH * DH)
    gains = gather_small(jnp.concatenate([gain_attn, gain_ffn, query_gain, key_gain]), me)
    w_qkv = lax.all_gather(
        jnp.concatenate([w_query, pair_shard], axis=1), "fsdp", axis=0, tiled=True
    )
    attn_gain = gains[:, :shard].reshape(D).astype(F32)
    ffn_gain = gains[:, shard : 2 * shard].reshape(D).astype(F32)
    q_gain = gains[:, 2 * shard : 2 * shard + head_shard].reshape(1, DH).astype(F32)
    k_gain = gains[:, 2 * shard + head_shard :].reshape(1, DH).astype(F32)

    unit = FF // count
    high = count // 4
    slot = me % 4
    parts_x = column_parts(w_gate, w_up, high, jnp.stack([me // 4, slot ^ 2, slot ^ 3]), 2)
    parts_own = column_parts(
        after(w_gate, parts_x), w_up, high, jnp.stack([me // 4, slot, slot ^ 1]), 2
    )
    got_x = swap(after(parts_x, w_qkv, gains), 2)
    wd = gather_rows(after(w_down, w_qkv, gains))
    out_pieces = [w_output]
    out_order = [0]
    bit = count // 2
    while bit > 2:
        out_pieces += [swap(piece, bit) for piece in out_pieces]
        out_order += [entry ^ bit for entry in out_order]
        bit //= 2
    out_block = jnp.concatenate(out_pieces, axis=0)
    cot_all = cotangent.reshape(total, D)

    freq = jnp.power(BASE, -jnp.arange(DH // 2, dtype=F32) / (DH // 2))
    angle = depths.reshape(total).astype(F32)[:, None] * freq[None, :]
    cosine = jnp.cos(angle)
    sine = jnp.sin(angle)
    cosine = jnp.concatenate([cosine, cosine], axis=1)
    sine = jnp.concatenate([-sine, sine], axis=1)
    masks = [
        visibility(parents[index, 0], layout[index, 0], offset, local) for index in range(micro)
    ]

    source = inputs.reshape(total, D).astype(F32)
    inv_in = inv_rms(source)
    normed_b = (source * inv_in * attn_gain).astype(BF)
    normed_now = after(normed_b, parts_own, out_block, *masks)
    got_core = swap(jnp.concatenate([parts_own[shard:], got_x[shard:]], axis=0), 1)
    pairs, pairs_raw = project(
        normed_now,
        w_qkv,
        QH * DH,
        2 * KVH * DH,
        cosine,
        sine,
        k_gain,
        "r-r-",
        "project_pairs",
    )
    everyone = [
        lax.all_gather(pairs[rows_of(index)], "ctx", axis=0, tiled=True) for index in range(micro)
    ]
    near = jnp.concatenate(
        [parts_own[:shard], got_core[:shard], got_x[:shard], got_core[shard:]], axis=0
    )
    queries, queries_raw = project(
        after(normed_b, pairs, near, wd),
        w_qkv,
        0,
        QH * DH,
        cosine,
        sine,
        q_gain,
        "rrrr",
        "project_queries",
    )
    pieces = [near] + [swap(near, 4 * far) for far in range(1, high)]
    for bit, earlier in ((2, queries), (1, everyone[0])):
        out_block = jnp.concatenate([out_block, swap(after(out_block, earlier), bit)], axis=0)
        out_order = out_order + [entry ^ bit for entry in out_order]
    w_out = jnp.zeros((QH * DH, D), BF)
    for index, entry in enumerate(out_order):
        w_out = lax.dynamic_update_slice_in_dim(
            w_out, out_block[index * shard : (index + 1) * shard], (me ^ entry) * shard, 0
        )
    cot_x = swap(after(cot_all, queries), 2)
    cot_rows = [cot_all, swap(cot_all, 1), cot_x, swap(cot_x, 1)]

    attended = []
    inverses = []
    middles = []
    mid_inverses = []
    mid_rows = []
    token = queries
    for index in range(micro):
        part = rows_of(index)
        if index == 0:
            token = (token,)
        else:
            token = (token, cot_x)
        out, inverse = attention(after(queries[part], *token), everyone[index], masks[index])
        middle = source[part] + mat(after(out, w_out) if index == 0 else out, w_out)
        inv_mid = inv_rms(middle)
        mid_b = (middle * inv_mid * ffn_gain).astype(BF)
        attended.append(out)
        inverses.append(inverse)
        middles.append(middle)
        mid_inverses.append(inv_mid)
        mid_rows.append(group_rows(mid_b))
        token = mid_b

    mid_pieces = [piece for rows in mid_rows for piece in rows]
    cot_pieces = [(piece, index) for index in range(micro) for piece in cot_rows]
    zero = jnp.zeros((1,), jnp.int32)

    def down_terms(act, far, added, cost=COST):
        return weight_terms(
            [act],
            zero + far,
            zero,
            unit,
            unit,
            cot_pieces,
            BLOCK,
            added,
            False,
            "grad_down",
            cost=cost,
        )

    def pair_terms(first, far, added, cost=COST):
        return weight_terms(
            [first] + mid_pieces[1:],
            ((me // 4) ^ far)[None],
            zero,
            D // high,
            D // high,
            [(dgu_b, 0)],
            unit,
            added,
            True,
            "grad_pair",
            2 * far,
            cost,
        )

    d_mids = []
    sent_pair = []
    me_array = me[None]
    act_b, dgu_b, wgu = feed(
        [after(mid_rows[0][0], token)] + mid_rows[0][1:],
        cot_rows,
        pieces,
        wd,
        0,
        micro,
        (),
        (me_array, unit),
    )
    for index in range(micro):
        if index:
            act_b, dgu_b = feed(
                [after(mid_rows[index][0], token)] + mid_rows[index][1:],
                cot_rows,
                [wgu],
                wd,
                index,
                micro,
                (act_b, dgu_b),
                (me_array, unit),
            )
        if index == micro - 1:
            token = act_b
            for far in range(1, high):
                sent_pair.append(pair_terms(after(mid_pieces[0], token), far, []))
                token = sent_pair[-1]
            dgu_now = after(dgu_b, token, d_mids[0][1])
        else:
            dgu_now = dgu_b
        parts = feed_out(dgu_now, wgu, index, (4, local), True, "feed_back")
        d_mids.append(group_half(parts))
        token = parts[0]
    got_pair = [swap(piece, 4 * (far + 1)) for far, piece in enumerate(sent_pair)]

    d_middles = []
    d_projs = []
    d_query_parts = []
    d_pair_parts = []
    d_ffn_gain = jnp.zeros((D,), F32)
    d_q_gain = jnp.zeros((1, DH), F32)
    for index in range(micro):
        part = rows_of(index)
        d_mid = d_mids[index][0] + swap(d_mids[index][1], 2).astype(F32)
        d_part, d_gain = rms_back(
            middles[index], mid_inverses[index], ffn_gain, after(d_mid, token)
        )
        d_ffn_gain = d_ffn_gain + d_gain
        d_middle = cotangent[index].astype(F32) + d_part
        d_proj = d_middle.astype(BF)
        d_attended = dot_last(d_proj, w_out).astype(BF)
        d_query, d_pair, d_gain = attention_back(
            after(queries[part], *[d_mids[later][1] for later in range(index + 1, micro)]),
            queries_raw[part],
            everyone[index],
            masks[index],
            d_attended,
            attended[index],
            inverses[index],
            cosine[part],
            sine[part],
            q_gain,
        )
        d_q_gain = d_q_gain + d_gain
        d_middles.append(d_middle)
        d_projs.append(d_proj)
        d_query_parts.append(d_query)
        d_pair_parts.append(scatter_ctx(d_pair))
        token = d_query
        if index == 0:
            sent_down = []
            for far in range(1, high):
                sent_down.append(down_terms(after(act_b, token), far, []))
                token = sent_down[-1]
            got_down = [swap(piece, 4 * (far + 1)) for far, piece in enumerate(sent_down)]

    d_query_b = jnp.concatenate(d_query_parts, axis=0)
    d_proj_b = jnp.concatenate(d_projs, axis=0)
    attended_b = jnp.concatenate(attended, axis=0)
    bits = [2**i for i in range(count.bit_length() - 1)]
    half_size = count // 2

    def plain_terms(left, right, order, added, name, cost=COST):
        starts = (me ^ jnp.array(order, jnp.int32)) * shard
        return weight_terms(
            [left], zero, starts, D, shard, [(right, 0)], BLOCK, added, False, name, cost=cost
        )

    order = order_of(bits)
    sent_query = plain_terms(after(normed_b, token), d_query_b, order[half_size:], [], "grad_q")
    sent_output = plain_terms(
        after(attended_b, sent_query), d_proj_b, order[half_size:], [], "grad_o"
    )

    outs = []
    token = sent_output
    for index in range(micro):
        parts = feed_out(after(act_b, token), wd, index, (4, local), False, "feed_forward")
        token = parts[0]
        outs.append((middles[index] + group_sum(parts)).astype(BF))
    outputs = jnp.stack(outs)

    own_pair = pair_terms(after(mid_pieces[0], token), 0, got_pair)
    own_down = down_terms(after(act_b, own_pair), 0, got_down, LOW)
    pair_piece = scatter_ctx(own_pair)
    down_piece = scatter_ctx(after(own_down, own_pair))
    own_query = plain_terms(
        after(normed_b, own_down, *d_pair_parts),
        d_query_b,
        order[:half_size],
        [swap(sent_query, 1)],
        "grad_q",
        LOW,
    )
    own_output = plain_terms(
        after(attended_b, own_query),
        d_proj_b,
        order[:half_size],
        [swap(sent_output, 1)],
        "grad_o",
        LOW,
    )

    d_pairs = after(jnp.concatenate(d_pair_parts, axis=0), own_output)
    d_pair_b, d_k_gain = pair_back(d_pairs, pairs_raw, cosine, sine, k_gain)
    sent_kv = plain_terms(normed_b, d_pair_b, order[half_size:], [], "grad_kv", LOW)
    d_normed = dot_last(
        jnp.concatenate([after(d_query_b, sent_kv), d_pair_b], axis=1), w_qkv
    )
    own_kv = plain_terms(
        after(normed_b, d_normed, pair_piece), d_pair_b, order[:half_size], [swap(sent_kv, 1)], "grad_kv"
    )
    d_source, d_attn_gain = rms_back(source, inv_in, attn_gain, after(d_normed, own_kv))
    grad_inputs = jnp.concatenate(d_middles, axis=0) + d_source

    def spread(vector):
        return jnp.pad(vector.reshape(count, -1), ((0, 0), (0, shard - vector.size // count)))

    columns = jnp.stack(
        [
            d_attn_gain.reshape(count, shard),
            d_ffn_gain.reshape(count, shard),
            spread(d_q_gain),
            spread(d_k_gain),
        ],
        axis=2,
    ).astype(BF)
    columns = jnp.pad(columns, ((0, 0), (0, 0), (0, DH - 4))).reshape(D, DH)
    columns = jnp.concatenate(
        [
            lax.dynamic_slice_in_dim(columns, (me ^ entry) * shard, shard, 0)
            for entry in order
        ],
        axis=0,
    )
    columns = fold(columns, bits[:1])
    part_qo = [fold(own, bits[1:2], own_kv) for own in (own_query, own_output)]
    part_qo = fold(jnp.concatenate(part_qo, axis=1), bits[2:])
    part_kv = fold(jnp.concatenate([own_kv, columns], axis=1), bits[1:])

    grad_gate, grad_up = spread_pairs(pair_piece, me, unit)

    def whole(piece):
        return lax.all_gather(piece, "ctx", axis=0, tiled=True).astype(F32)

    grad_down = whole(down_piece)
    both = whole(scatter_ctx(part_qo))
    grad_query, grad_output = both[:, :D], both[:, D:]
    rest = whole(scatter_ctx(part_kv))
    pair_both = rest[:, : 2 * KVH * DH].reshape(shard, KVH, 2, DH)
    grad_key = pair_both[:, :, 0].reshape(shard, KVH * DH)
    grad_value = pair_both[:, :, 1].reshape(shard, KVH * DH)
    sums = rest[:, 2 * KVH * DH :]

    return (
        outputs,
        grad_inputs.reshape(micro, local, D),
        sums[:, 0],
        grad_query,
        grad_key,
        grad_value,
        sums[:head_shard, 2],
        sums[:head_shard, 3],
        grad_output,
        sums[:, 1],
        grad_gate,
        grad_up,
        grad_down,
    )


def solution(mesh):
    rows = P(None, ("fsdp", "ctx"), None)
    tree = P(None, "fsdp", None)
    vector = P("fsdp")
    weight = P("fsdp", None)
    in_specs = (
        rows,
        P(None, ("fsdp", "ctx")),
        tree,
        tree,
        vector,
        weight,
        weight,
        weight,
        vector,
        vector,
        weight,
        vector,
        weight,
        weight,
        weight,
        rows,
    )
    out_specs = (
        rows,
        rows,
        vector,
        weight,
        weight,
        weight,
        vector,
        vector,
        weight,
        vector,
        weight,
        weight,
        weight,
    )
    return jax.shard_map(body, mesh=mesh, in_specs=in_specs, out_specs=out_specs, check_vma=False)
```

```python
import functools

import jax
import jax.numpy as jnp
from jax import lax
from jax.experimental import pallas as pl
from jax.experimental.pallas import tpu as pltpu
from jax.sharding import PartitionSpec as P

D = 2048
QH = 16
KVH = 8
DH = 128
FF = 6144
BLK = 128
GROUP = QH // KVH
SCALE = DH ** (-0.5)
LOG2E = 1.4426950408889634

EPS = 1e-06
BASE = 1000000.0
BF = jnp.bfloat16
F32 = jnp.float32
BLOCK = 512
COST = 100.0
LOW = 45.0
VMEM = 60 * 1024 * 1024


def mat(left, right):
    return jnp.dot(left, right, preferred_element_type=F32)


def dot_last(left, right):
    return lax.dot_general(left, right, (((1,), (1,)), ((), ())), preferred_element_type=F32)


def outer(left, right):
    return lax.dot_general(left, right, (((0,), (0,)), ((), ())), preferred_element_type=F32)


def after(value, *others):
    return lax.optimization_barrier((value,) + others)[0]


def swap(value, bits):
    count = lax.axis_size("fsdp")
    return lax.ppermute(value, "fsdp", [(i, i ^ bits) for i in range(count)])


def inv_rms(values):
    return lax.rsqrt(jnp.mean(values * values, axis=-1, keepdims=True) + EPS)


def rms_back(values, inv, gain, dy):
    product = dy * values
    dv = inv * (gain * dy) - values * (inv * inv * inv) * jnp.mean(
        product * gain, axis=-1, keepdims=True
    )
    return dv, jnp.sum(product * inv, axis=0)


def call(
    kernel,
    name,
    grid,
    in_specs,
    out_specs,
    out_shape,
    flops,
    moved,
    scratch=(),
    aliases=None,
    scalars=0,
    cost=COST,
):
    return pl.pallas_call(
        kernel,
        name=name,
        grid_spec=pltpu.PrefetchScalarGridSpec(
            num_scalar_prefetch=scalars,
            grid=grid,
            in_specs=in_specs,
            out_specs=out_specs,
            scratch_shapes=list(scratch),
        ),
        out_shape=out_shape,
        input_output_aliases=aliases or {},
        compiler_params=pltpu.CompilerParams(vmem_limit_bytes=VMEM),
        cost_estimate=pl.CostEstimate(
            flops=int(flops * cost), bytes_accessed=int(moved * cost), transcendentals=0
        ),
    )


def fixed(shape):
    return pl.BlockSpec(
        shape, lambda *index: tuple(0 for _ in shape), pipeline_mode=pl.Buffered(1)
    )


def project(x, weight, first, cols, cosine, sine, gain, kinds, name, cost=COST):
    rows, depth = x.shape
    width = DH * len(kinds)

    def kernel(x_ref, w_ref, c_ref, s_ref, g_ref, out_ref, raw_ref):
        raw = mat(x_ref[...], w_ref[...])
        raw_ref[...] = raw.astype(BF)
        for index, kind in enumerate(kinds):
            part = raw[:, index * DH : (index + 1) * DH]
            if kind == "r":
                part = part * inv_rms(part) * g_ref[...]
                part = part * c_ref[...] + pltpu.roll(part, DH // 2, 1) * s_ref[...]
            out_ref[:, index * DH : (index + 1) * DH] = part.astype(BF)

    whole = lambda j: (0, 0)
    block = lambda j: (0, j)
    return call(
        kernel,
        name,
        (cols // width,),
        [
            pl.BlockSpec((rows, depth), whole),
            pl.BlockSpec((depth, width), lambda j: (0, j + first // width)),
            pl.BlockSpec((rows, DH), whole),
            pl.BlockSpec((rows, DH), whole),
            pl.BlockSpec((1, DH), whole),
        ],
        [pl.BlockSpec((rows, width), block)] * 2,
        [jax.ShapeDtypeStruct((rows, cols), BF)] * 2,
        2 * rows * depth * cols,
        2 * (rows * depth + depth * cols + 2 * rows * cols),
        cost=cost,
    )(x, weight, cosine, sine, gain)


def stack_heads(block):
    return jnp.concatenate([block[:, i * DH : (i + 1) * DH] for i in range(GROUP)], axis=0)


def attention(queries, pairs, mask):
    rows = queries.shape[0]
    keys = pairs.shape[0]

    def kernel(q_ref, kv_ref, m_ref, out_ref, inv_ref):
        stacked = stack_heads(q_ref[...])
        scores = dot_last(kv_ref[:, :DH], stacked)
        mask_now = jnp.concatenate([m_ref[...]] * GROUP, axis=1)
        powers = jnp.exp2(scores * (SCALE * LOG2E)) * mask_now
        inv = 1.0 / jnp.sum(powers, axis=0, keepdims=True)
        inv_ref[0] = inv
        out = (outer(kv_ref[:, DH:], powers.astype(BF)) * inv).T
        for index in range(GROUP):
            out_ref[:, index * DH : (index + 1) * DH] = out[
                index * rows : (index + 1) * rows
            ].astype(BF)

    return call(
        kernel,
        "attention",
        (KVH,),
        [
            pl.BlockSpec((rows, GROUP * DH), lambda g: (0, g)),
            pl.BlockSpec((keys, 2 * DH), lambda g: (0, g)),
            pl.BlockSpec((keys, rows), lambda g: (0, 0)),
        ],
        [
            pl.BlockSpec((rows, GROUP * DH), lambda g: (0, g)),
            pl.BlockSpec((1, 1, GROUP * rows), lambda g: (g, 0, 0)),
        ],
        [
            jax.ShapeDtypeStruct((rows, QH * DH), BF),
            jax.ShapeDtypeStruct((KVH, 1, GROUP * rows), F32),
        ],
        4 * QH * rows * keys * DH,
        2 * (2 * rows * QH * DH + 2 * keys * KVH * DH),
    )(queries, pairs, mask)


def head_back(dy, raw, cosine, sine, gain):
    turned = dy * cosine - pltpu.roll(dy, DH // 2, 1) * sine
    inv = inv_rms(raw)
    product = turned * raw
    dv = inv * (gain * turned) - raw * (inv * inv * inv) * jnp.mean(
        product * gain, axis=-1, keepdims=True
    )
    return dv, jnp.sum(product * inv, axis=0, keepdims=True)


def attention_back(queries, raw, pairs, mask, d_out, out, inv, cosine, sine, gain):
    rows = queries.shape[0]
    keys = pairs.shape[0]

    def kernel(
        q_ref, r_ref, kv_ref, m_ref, do_ref, o_ref, inv_ref, c_ref, s_ref, g_ref,
        dq_ref, dkv_ref, dg_ref,
    ):
        stacked = stack_heads(q_ref[...])
        d_stacked = stack_heads(do_ref[...])
        o_stacked = stack_heads(o_ref[...])
        dots = jnp.sum((d_stacked.astype(F32) * o_stacked.astype(F32)).T, axis=0, keepdims=True)
        scores = dot_last(kv_ref[:, :DH], stacked)
        mask_now = jnp.concatenate([m_ref[...]] * GROUP, axis=1)
        probs = jnp.exp2(scores * (SCALE * LOG2E)) * (mask_now * inv_ref[0])
        d_probs = dot_last(kv_ref[:, DH:], d_stacked)
        d_scores = (probs * (d_probs - dots)).astype(BF)
        dkv_ref[:, DH:] = mat(probs.astype(BF), d_stacked).astype(BF)
        dkv_ref[:, :DH] = (mat(d_scores, stacked) * SCALE).astype(BF)
        d_query = outer(d_scores, kv_ref[:, :DH]) * SCALE
        total = jnp.zeros((1, DH), F32)
        for index in range(GROUP):
            part = slice(index * DH, (index + 1) * DH)
            dv, dg = head_back(
                d_query[index * rows : (index + 1) * rows],
                r_ref[:, part].astype(F32),
                c_ref[...],
                s_ref[...],
                g_ref[...],
            )
            dq_ref[:, part] = dv.astype(BF)
            total = total + dg

        @pl.when(pl.program_id(0) == 0)
        def _():
            dg_ref[...] = jnp.zeros_like(dg_ref)

        dg_ref[...] += total

    head = pl.BlockSpec((rows, GROUP * DH), lambda g: (0, g))
    pair = pl.BlockSpec((keys, 2 * DH), lambda g: (0, g))
    whole = lambda shape: pl.BlockSpec(shape, lambda g: (0, 0))
    return call(
        kernel,
        "attention_back",
        (KVH,),
        [
            head,
            head,
            pair,
            whole((keys, rows)),
            head,
            head,
            pl.BlockSpec((1, 1, GROUP * rows), lambda g: (g, 0, 0)),
            whole((rows, DH)),
            whole((rows, DH)),
            whole((1, DH)),
        ],
        [head, pair, whole((1, DH))],
        [
            jax.ShapeDtypeStruct((rows, QH * DH), BF),
            jax.ShapeDtypeStruct((keys, 2 * KVH * DH), BF),
            jax.ShapeDtypeStruct((1, DH), F32),
        ],
        10 * QH * rows * keys * DH,
        2 * (5 * rows * QH * DH + 4 * keys * KVH * DH),
    )(queries, raw, pairs, mask, d_out, out, inv, cosine, sine, gain)


def pair_back(d_pairs, raw, cosine, sine, gain):
    rows, cols = d_pairs.shape

    def kernel(d_ref, r_ref, c_ref, s_ref, g_ref, out_ref, dg_ref):
        total = jnp.zeros((1, DH), F32)
        for index in range(BLOCK // (2 * DH)):
            part = slice(index * 2 * DH, index * 2 * DH + DH)
            rest = slice(index * 2 * DH + DH, (index + 1) * 2 * DH)
            dv, dg = head_back(
                d_ref[:, part].astype(F32),
                r_ref[:, part].astype(F32),
                c_ref[...],
                s_ref[...],
                g_ref[...],
            )
            out_ref[:, part] = dv.astype(BF)
            out_ref[:, rest] = d_ref[:, rest]
            total = total + dg

        @pl.when(pl.program_id(0) == 0)
        def _():
            dg_ref[...] = jnp.zeros_like(dg_ref)

        dg_ref[...] += total

    block = pl.BlockSpec((rows, BLOCK), lambda j: (0, j))
    whole = lambda shape: pl.BlockSpec(shape, lambda j: (0, 0))
    return call(
        kernel,
        "pair_back",
        (cols // BLOCK,),
        [block, block, whole((rows, DH)), whole((rows, DH)), whole((1, DH))],
        [block, whole((1, DH))],
        [jax.ShapeDtypeStruct((rows, cols), BF), jax.ShapeDtypeStruct((1, DH), F32)],
        20 * rows * cols,
        6 * rows * cols,
        cost=LOW,
    )(d_pairs, raw, cosine, sine, gain)


def feed(mids, cots, pieces, w_down, index, total, earlier, place):
    rows, depth = mids[0].shape
    parts = len(mids)
    hidden = w_down.shape[0]
    count = len(pieces)
    unit = place[1]
    steps = hidden // unit
    block_rows = depth // (4 * count)

    def kernel(me_ref, *refs):
        mid_refs = refs[:parts]
        cot_refs = refs[parts : 2 * parts]
        piece_refs = refs[2 * parts : 2 * parts + count]
        wd_ref = refs[2 * parts + count]
        if count > 1:
            act_ref, d_ref, wp_ref = refs[-3:]
            for which in range(4 * count):
                start = pl.multiple_of((me_ref[0] ^ which) * block_rows, block_rows)
                near = which % 4 * block_rows
                wp_ref[pl.ds(start, block_rows), :] = piece_refs[which // 4][
                    near : near + block_rows
                ]
        else:
            act_ref, d_ref = refs[-2:]
            wp_ref = piece_refs[0]
        for part in range(parts):
            now = slice(part * rows, (part + 1) * rows)
            both = mat(mid_refs[part][...], wp_ref[...])
            gate = both[:, :unit]
            up = both[:, unit:]
            d_act = dot_last(cot_refs[part][...], wd_ref[...])
            sig = 1.0 / (1.0 + jnp.exp2(gate * (-LOG2E)))
            silu = gate * sig
            act_ref[now] = (silu * up).astype(BF)
            d_ref[now, unit:] = (d_act * silu).astype(BF)
            d_ref[now, :unit] = (d_act * up * (sig + silu * (1.0 - sig))).astype(BF)

    def piece_spec(far):
        return pl.BlockSpec((pieces[0].shape[0], 2 * unit), lambda j, me: (0, j ^ far))

    out_specs = [
        pl.BlockSpec((parts * rows, unit), lambda j, me: (index, j)),
        pl.BlockSpec((parts * rows, 2 * unit), lambda j, me: (index, j)),
    ]
    out_shape = [
        jax.ShapeDtypeStruct((total * parts * rows, hidden), BF),
        jax.ShapeDtypeStruct((total * parts * rows, 2 * hidden), BF),
    ]
    if count > 1:
        out_specs.append(pl.BlockSpec((depth, 2 * unit), lambda j, me: (0, j)))
        out_shape.append(jax.ShapeDtypeStruct((depth, 2 * hidden), BF))
    before = 1 + 2 * parts + count + 1
    return call(
        kernel,
        "feed",
        (steps,),
        [fixed((rows, depth))] * parts
        + [
            pl.BlockSpec(
                (rows, depth), lambda j, me: (index, 0), pipeline_mode=pl.Buffered(1)
            )
        ]
        * parts
        + [piece_spec(which) for which in range(count)]
        + [pl.BlockSpec((unit, depth), lambda j, me: (j, 0))]
        + [pl.BlockSpec(memory_space=pl.ANY)] * len(earlier),
        out_specs,
        out_shape,
        6 * parts * rows * depth * hidden,
        2 * (2 * parts * rows * depth + 3 * depth * hidden + 3 * parts * rows * hidden),
        aliases={before + i: i for i in range(len(earlier))},
        scalars=1,
    )(place[0], *mids, *cots, *pieces, w_down, *earlier)


def feed_out(left, weight, index, parts, transposed, name, dtype=BF):
    depth = left.shape[1]
    cols = weight.shape[0] if transposed else weight.shape[1]
    rows = parts[1]

    def kernel(a_ref, w_ref, *outs):
        for part in range(parts[0]):
            now = a_ref[part * rows : (part + 1) * rows]
            result = dot_last(now, w_ref[...]) if transposed else mat(now, w_ref[...])
            outs[part][...] = result.astype(dtype)

    return call(
        kernel,
        name,
        (cols // BLOCK,),
        [
            pl.BlockSpec((parts[0] * rows, depth), lambda j: (index, 0)),
            pl.BlockSpec((BLOCK, depth), lambda j: (j, 0))
            if transposed
            else pl.BlockSpec((depth, BLOCK), lambda j: (0, j)),
        ],
        [pl.BlockSpec((rows, BLOCK), lambda j: (0, j))] * parts[0],
        [jax.ShapeDtypeStruct((rows, cols), dtype)] * parts[0],
        2 * parts[0] * rows * depth * cols,
        2 * (parts[0] * rows * (depth + cols) + depth * cols),
    )(left, weight)


def weight_terms(lefts, block, starts, width, size, rights, step, added, chunked, name, turn=0, cost=COST):
    depth = sum(left.shape[0] for left in lefts)
    cols = rights[0][0].shape[1]
    size_right = depth // len(rights)
    blocks = starts.shape[0]
    rows = blocks * size
    steps = cols // step
    nl, nr = len(lefts), len(rights)

    def kernel(block_ref, start_ref, *refs):
        left_refs = refs[:nl]
        right_refs = refs[nl : nl + nr]
        add_refs = refs[nl + nr : nl + nr + len(added)]
        out_ref, turned = refs[-2:]

        @pl.when(pl.program_id(0) == 0)
        def _():
            for which in range(blocks):
                start = pl.multiple_of(start_ref[which], 128)
                at = 0
                for ref in left_refs:
                    turned[which * size : (which + 1) * size, at : at + ref.shape[0]] = ref[
                        :, pl.ds(start, size)
                    ].T
                    at += ref.shape[0]

        right = [ref[...] for ref in right_refs]
        right = right[0] if nr == 1 else jnp.concatenate(right, axis=0)
        result = mat(turned[...], right)
        for ref in add_refs:
            result = result + ref[...].astype(F32)
        out_ref[...] = result.astype(BF)

    if chunked:
        out_spec = pl.BlockSpec((rows, step), lambda j, b, s: (j ^ turn, 0))
        shape = (steps * rows, step)
    else:
        out_spec = pl.BlockSpec((rows, step), lambda j, b, s: (0, j))
        shape = (rows, cols)
    return call(
        kernel,
        name,
        (steps,),
        [
            pl.BlockSpec(
                (left.shape[0], width), lambda j, b, s: (0, b[0]), pipeline_mode=pl.Buffered(1)
            )
            for left in lefts
        ]
        + [
            pl.BlockSpec((size_right, step), functools.partial(lambda at, j, b, s: (at, j), at))
            for right, at in rights
        ]
        + [out_spec] * len(added),
        out_spec,
        jax.ShapeDtypeStruct(shape, BF),
        2 * rows * depth * cols,
        2 * (rows * depth + depth * cols + (1 + len(added)) * rows * cols),
        scratch=[pltpu.VMEM((rows, depth), BF)],
        scalars=2,
        cost=cost,
    )(block, starts, *lefts, *[right for right, at in rights], *added)


def column_parts(gate, up, high, slots, number):
    rows, cols = gate.shape
    unit = cols // (4 * high)

    def kernel(slot_ref, gate_ref, up_ref, out_ref):
        out_ref[:, :unit] = gate_ref[...]
        out_ref[:, unit:] = up_ref[...]

    block = pl.BlockSpec((rows, unit), lambda i, j, at: (0, (at[0] ^ j) * 4 + at[i + 1]))
    return call(
        kernel,
        "column_parts",
        (number, high),
        [block, block],
        pl.BlockSpec((rows, 2 * unit), lambda i, j, at: (i, j)),
        jax.ShapeDtypeStruct((number * rows, 2 * unit * high), BF),
        0,
        8 * number * rows * unit * high,
        scalars=1,
    )(slots, gate, up)


def lay_pairs(chunks, place, high, unit):
    depth = len(chunks)
    rows = chunks[0].shape[1]
    cols = 4 * high * unit
    size = rows // 4

    def kernel(place_ref, *refs):
        gate_ref, up_ref = refs[-2:]
        for which in range(depth):
            chunk = place_ref[0] ^ which
            far = place_ref[1] ^ (chunk // 2)
            for near in range(4):
                start = pl.multiple_of((far * 4 + (place_ref[2] ^ near)) * unit, 128)

                @pl.when(chunk % 2 == 0)
                def _():
                    gate_ref[:, pl.ds(start, unit)] = refs[which][near].astype(F32)

                @pl.when(chunk % 2 == 1)
                def _():
                    up_ref[:, pl.ds(start, unit)] = refs[which][near].astype(F32)

    return call(
        kernel,
        "lay_pairs",
        (4,),
        [pl.BlockSpec((4, size, unit), lambda i, at: (0, i, 0))] * depth,
        [pl.BlockSpec((size, cols), lambda i, at: (i, 0))] * 2,
        [jax.ShapeDtypeStruct((rows, cols), F32)] * 2,
        0,
        12 * rows * cols,
        scalars=1,
    )(place, *chunks)


def visibility(parent, layout, offset, count):
    blocks = parent.shape[0]
    ident = jnp.arange(blocks, dtype=jnp.int32)
    current = ident
    reach = ident[:, None] == ident[None, :]
    for step in range(blocks):
        current = jnp.sum(jnp.where(current[:, None] == ident[None, :], parent[None, :], 0), axis=1)
        reach = reach | (current[:, None] == ident[None, :])
    place = (layout[:, None] == ident[None, :]).astype(jnp.int32)
    picked = jnp.sum(place[:, :, None] * reach.astype(jnp.int32)[None, :, :], axis=1)
    row_reach = jnp.sum(picked[:, None, :] * place[None, :, :], axis=2) > 0
    mine = lax.dynamic_slice_in_dim(row_reach, offset // BLK, count // BLK, 0).T
    spread = jnp.broadcast_to(
        mine[:, None, :, None], (blocks, BLK, count // BLK, BLK)
    ).reshape(blocks * BLK, count)
    query_rows = offset + lax.broadcasted_iota(jnp.int32, (blocks * BLK, count), 1)
    key_rows = lax.broadcasted_iota(jnp.int32, (blocks * BLK, count), 0)
    same = query_rows // BLK == key_rows // BLK
    return (spread & (jnp.logical_not(same) | (key_rows <= query_rows))).astype(F32)


def gather_small(vector, me):
    count = lax.axis_size("fsdp")
    buffer = jnp.zeros((count,) + vector.shape, vector.dtype)
    buffer = lax.dynamic_update_index_in_dim(buffer, vector, me, 0)
    step = 1
    while step < count:
        buffer = buffer + swap(buffer, step)
        step *= 2
    return buffer


def gather_rows(shard):
    high = lax.axis_size("fsdp") // 4
    return jnp.concatenate(
        [shard] + [swap(shard, 4 * far) for far in range(1, high)], axis=0
    )


def group_rows(rows):
    from_x = swap(rows, 2)
    from_core = swap(rows, 1)
    from_both = swap(from_x, 1)
    return [rows, from_core, from_x, from_both]


def group_half(parts):
    got = swap(jnp.concatenate([parts[1], parts[3]], axis=0), 1)
    rows = parts[0].shape[0]
    own = parts[0].astype(F32) + got[:rows].astype(F32)
    return own, (parts[2].astype(F32) + got[rows:].astype(F32)).astype(BF)


def gather_ctx(chunk):
    count = lax.axis_size("ctx")
    return [chunk] + [
        lax.ppermute(chunk, "ctx", [(i, i ^ step) for i in range(count)])
        for step in range(1, count)
    ]


def scatter_ctx(array):
    return lax.psum_scatter(array, "ctx", scatter_dimension=0, tiled=True)


def spread_near(piece, me):
    slot = me % 4
    rows = piece.shape[0] // 4
    near = [lax.dynamic_slice_in_dim(piece, (slot ^ which) * rows, rows, 0) for which in range(4)]
    return near, jnp.stack([near[0]] + [swap(near[which], which) for which in range(1, 4)])


def fold(value, bits, *others):
    for bit in bits:
        half = value.shape[0] // 2
        got = swap(value[half:], bit)
        keep = after(value[:half], *others) if others else value[:half]
        value = (keep.astype(F32) + got.astype(F32)).astype(BF)
        others = ()
    return value


def order_of(bits):
    order = [0]
    for bit in reversed(bits):
        order = order + [entry ^ bit for entry in order]
    return order


def body(
    inputs,
    depths,
    parents,
    layout,
    gain_attn,
    w_query,
    w_key,
    w_value,
    query_gain,
    key_gain,
    w_output,
    gain_ffn,
    w_gate,
    w_up,
    w_down,
    cotangent,
):
    me = lax.axis_index("fsdp")
    micro, local, _ = inputs.shape
    total = micro * local
    offset = lax.axis_index("ctx") * local
    count = lax.axis_size("fsdp")
    shard = D // count
    head_shard = DH // count

    def rows_of(index):
        return slice(index * local, (index + 1) * local)

    pair_shard = jnp.stack(
        [w_key.reshape(shard, KVH, DH), w_value.reshape(shard, KVH, DH)], axis=2
    ).reshape(shard, 2 * KVH * DH)
    gains = gather_small(jnp.concatenate([gain_attn, gain_ffn, query_gain, key_gain]), me)
    w_qkv = lax.all_gather(
        jnp.concatenate([w_query, pair_shard], axis=1), "fsdp", axis=0, tiled=True
    )
    attn_gain = gains[:, :shard].reshape(D).astype(F32)
    ffn_gain = gains[:, shard : 2 * shard].reshape(D).astype(F32)
    q_gain = gains[:, 2 * shard : 2 * shard + head_shard].reshape(1, DH).astype(F32)
    k_gain = gains[:, 2 * shard + head_shard :].reshape(1, DH).astype(F32)

    unit = FF // count
    high = count // 4
    slot = me % 4
    parts_x = column_parts(w_gate, w_up, high, jnp.stack([me // 4, slot ^ 2, slot ^ 3]), 2)
    parts_own = column_parts(
        after(w_gate, parts_x), w_up, high, jnp.stack([me // 4, slot, slot ^ 1]), 2
    )
    got_x = swap(after(parts_x, w_qkv, gains), 2)
    wd = gather_rows(after(w_down, w_qkv, gains))
    out_pieces = [w_output]
    out_order = [0]
    bit = count // 2
    while bit > 2:
        out_pieces += [swap(piece, bit) for piece in out_pieces]
        out_order += [entry ^ bit for entry in out_order]
        bit //= 2
    out_block = jnp.concatenate(out_pieces, axis=0)
    cot_all = cotangent.reshape(total, D)

    freq = jnp.power(BASE, -jnp.arange(DH // 2, dtype=F32) / (DH // 2))
    angle = depths.reshape(total).astype(F32)[:, None] * freq[None, :]
    cosine = jnp.cos(angle)
    sine = jnp.sin(angle)
    cosine = jnp.concatenate([cosine, cosine], axis=1)
    sine = jnp.concatenate([-sine, sine], axis=1)
    masks = [
        visibility(parents[index, 0], layout[index, 0], offset, local) for index in range(micro)
    ]

    source = inputs.reshape(total, D).astype(F32)
    inv_in = inv_rms(source)
    normed_b = (source * inv_in * attn_gain).astype(BF)
    normed_now = after(normed_b, parts_own, out_block, *masks)
    pairs, pairs_raw = project(
        normed_now,
        w_qkv,
        QH * DH,
        2 * KVH * DH,
        cosine,
        sine,
        k_gain,
        "r-r-",
        "project_pairs",
    )
    everyone = [
        lax.all_gather(pairs[rows_of(index)], "ctx", axis=0, tiled=True) for index in range(micro)
    ]
    got_core = swap(
        jnp.concatenate([parts_own[shard:], after(got_x, pairs, wd)[shard:]], axis=0), 1
    )
    near = jnp.concatenate(
        [parts_own[:shard], got_core[:shard], got_x[:shard], got_core[shard:]], axis=0
    )
    queries, queries_raw = project(
        after(normed_b, pairs, near, wd),
        w_qkv,
        0,
        QH * DH,
        cosine,
        sine,
        q_gain,
        "rrrr",
        "project_queries",
        0.01,
    )
    pieces = [near] + [swap(near, 4 * far) for far in range(1, high)]
    for bit, earlier in ((2, near), (1, everyone[0])):
        out_block = jnp.concatenate([out_block, swap(after(out_block, earlier), bit)], axis=0)
        out_order = out_order + [entry ^ bit for entry in out_order]
    w_out = jnp.zeros((QH * DH, D), BF)
    for index, entry in enumerate(out_order):
        w_out = lax.dynamic_update_slice_in_dim(
            w_out, out_block[index * shard : (index + 1) * shard], (me ^ entry) * shard, 0
        )
    cot_x = swap(after(cot_all, near), 2)
    cot_rows = [cot_all, swap(cot_all, 1), cot_x, swap(cot_x, 1)]

    attended = []
    inverses = []
    middles = []
    mid_inverses = []
    mid_rows = []
    token = queries
    for index in range(micro):
        part = rows_of(index)
        if index == 0:
            token = (token,)
        else:
            token = (token, cot_x)
        out, inverse = attention(after(queries[part], *token), everyone[index], masks[index])
        middle = source[part] + mat(after(out, w_out) if index == 0 else out, w_out)
        inv_mid = inv_rms(middle)
        mid_b = (middle * inv_mid * ffn_gain).astype(BF)
        attended.append(out)
        inverses.append(inverse)
        middles.append(middle)
        mid_inverses.append(inv_mid)
        mid_rows.append(group_rows(mid_b))
        token = mid_b

    mid_pieces = [piece for rows in mid_rows for piece in rows]
    cot_pieces = [(piece, index) for index in range(micro) for piece in cot_rows]
    zero = jnp.zeros((1,), jnp.int32)

    def down_terms(act, far, added, cost=COST):
        return weight_terms(
            [act],
            zero + far,
            zero,
            unit,
            unit,
            cot_pieces,
            BLOCK,
            added,
            False,
            "grad_down",
            cost=cost,
        )

    def pair_terms(first, far, added, cost=COST):
        return weight_terms(
            [first] + mid_pieces[1:],
            ((me // 4) ^ far)[None],
            zero,
            D // high,
            D // high,
            [(dgu_b, 0)],
            unit,
            added,
            True,
            "grad_pair",
            2 * far,
            cost,
        )

    d_mids = []
    me_array = me[None]
    act_b, dgu_b, wgu = feed(
        [after(mid_rows[0][0], token)] + mid_rows[0][1:],
        cot_rows,
        pieces,
        wd,
        0,
        micro,
        (),
        (me_array, unit),
    )
    for index in range(micro):
        if index:
            act_b, dgu_b = feed(
                [after(mid_rows[index][0], token)] + mid_rows[index][1:],
                cot_rows,
                [wgu],
                wd,
                index,
                micro,
                (act_b, dgu_b),
                (me_array, unit),
            )
        parts = feed_out(
            after(dgu_b, act_b, *[d_mid[1] for d_mid in d_mids]),
            wgu,
            index,
            (4, local),
            True,
            "feed_back",
        )
        d_mids.append(group_half(parts))
        token = parts[0]
    sent_pair = []
    for far in range(1, high):
        sent_pair.append(pair_terms(after(mid_pieces[0], token), far, []))
        token = sent_pair[-1]
    got_pair = [swap(piece, 4 * (far + 1)) for far, piece in enumerate(sent_pair)]

    d_middles = []
    d_projs = []
    d_query_parts = []
    d_pair_parts = []
    d_ffn_gain = jnp.zeros((D,), F32)
    d_q_gain = jnp.zeros((1, DH), F32)
    for index in range(micro):
        part = rows_of(index)
        d_mid = d_mids[index][0] + swap(d_mids[index][1], 2).astype(F32)
        d_part, d_gain = rms_back(
            middles[index], mid_inverses[index], ffn_gain, after(d_mid, token)
        )
        d_ffn_gain = d_ffn_gain + d_gain
        d_middle = cotangent[index].astype(F32) + d_part
        d_proj = d_middle.astype(BF)
        d_attended = dot_last(d_proj, w_out).astype(BF)
        d_query, d_pair, d_gain = attention_back(
            after(queries[part], *[d_mids[later][1] for later in range(index + 1, micro)]),
            queries_raw[part],
            everyone[index],
            masks[index],
            d_attended,
            attended[index],
            inverses[index],
            cosine[part],
            sine[part],
            q_gain,
        )
        d_q_gain = d_q_gain + d_gain
        d_middles.append(d_middle)
        d_projs.append(d_proj)
        d_query_parts.append(d_query)
        d_pair_parts.append(scatter_ctx(d_pair))
        token = d_query
        if index == 0:
            sent_down = []
            for far in range(1, high):
                sent_down.append(down_terms(after(act_b, token), far, []))
                token = sent_down[-1]
            got_down = [swap(piece, 4 * (far + 1)) for far, piece in enumerate(sent_down)]

    d_query_b = jnp.concatenate(d_query_parts, axis=0)
    d_proj_b = jnp.concatenate(d_projs, axis=0)
    attended_b = jnp.concatenate(attended, axis=0)
    bits = [2**i for i in range(count.bit_length() - 1)]
    half_size = count // 2

    def plain_terms(left, right, order, added, name, cost=COST):
        starts = (me ^ jnp.array(order, jnp.int32)) * shard
        return weight_terms(
            [left], zero, starts, D, shard, [(right, 0)], BLOCK, added, False, name, cost=cost
        )

    order = order_of(bits)
    out_parts = []
    for index in range(micro):
        out_parts.append(
            feed_out(after(act_b, token), wd, index, (4, local), False, "feed_forward")
        )
        token = out_parts[-1][0]
    out_half = group_half([jnp.concatenate(list(pair), axis=0) for pair in zip(*out_parts)])
    sent_query = plain_terms(after(normed_b, token), d_query_b, order[half_size:], [], "grad_q")
    sent_output = plain_terms(
        after(attended_b, sent_query), d_proj_b, order[half_size:], [], "grad_o"
    )
    own_pair = pair_terms(after(mid_pieces[0], sent_output, out_half[1]), 0, got_pair)
    own_query = plain_terms(
        after(normed_b, own_pair), d_query_b, order[:half_size], [swap(sent_query, 1)], "grad_q"
    )
    own_output = plain_terms(
        after(attended_b, own_query), d_proj_b, order[:half_size], [swap(sent_output, 1)], "grad_o"
    )
    own_down = down_terms(after(act_b, own_output), 0, got_down)
    outputs = jnp.concatenate(middles, axis=0) + out_half[0]
    outputs = (outputs + swap(out_half[1], 2).astype(F32)).astype(BF).reshape(micro, local, D)
    pair_piece = scatter_ctx(own_pair)
    down_piece = scatter_ctx(after(own_down, own_pair))

    d_pairs = after(jnp.concatenate(d_pair_parts, axis=0), own_down, outputs)
    d_pair_b, d_k_gain = pair_back(d_pairs, pairs_raw, cosine, sine, k_gain)
    part_qo = [fold(own_query, bits[1:2], d_pair_b), fold(own_output, bits[1:2], d_pair_b)]
    sent_kv = plain_terms(after(normed_b, *part_qo), d_pair_b, order[half_size:], [], "grad_kv", LOW)
    (d_normed,) = feed_out(
        jnp.concatenate([after(d_query_b, sent_kv), d_pair_b], axis=1),
        w_qkv,
        0,
        (1, total),
        True,
        "d_normed",
        F32,
    )
    own_kv = plain_terms(
        after(normed_b, d_normed), d_pair_b, order[:half_size], [swap(sent_kv, 1)], "grad_kv"
    )
    d_source, d_attn_gain = rms_back(source, inv_in, attn_gain, after(d_normed, own_kv))
    grad_inputs = jnp.concatenate(d_middles, axis=0) + d_source

    def spread(vector):
        return jnp.pad(vector.reshape(count, -1), ((0, 0), (0, shard - vector.size // count)))

    columns = jnp.stack(
        [
            d_attn_gain.reshape(count, shard),
            d_ffn_gain.reshape(count, shard),
            spread(d_q_gain),
            spread(d_k_gain),
        ],
        axis=2,
    ).astype(BF)
    columns = jnp.pad(columns, ((0, 0), (0, 0), (0, DH - 4))).reshape(D, DH)
    columns = jnp.concatenate(
        [
            lax.dynamic_slice_in_dim(columns, (me ^ entry) * shard, shard, 0)
            for entry in order
        ],
        axis=0,
    )
    columns = fold(columns, bits[:1])
    near_parts, pair_near = spread_near(pair_piece, me)
    chunks = gather_ctx(pair_near)
    down_whole = lax.all_gather(down_piece, "ctx", axis=0, tiled=True)
    part_qo = fold(jnp.concatenate(part_qo, axis=1), bits[2:])
    part_kv = fold(
        jnp.concatenate([after(own_kv, *near_parts), columns], axis=1), bits[1:2], pair_near
    )
    part_kv = fold(part_kv, bits[2:])

    grad_gate, grad_up = lay_pairs(
        chunks, jnp.stack([lax.axis_index("ctx"), me // 4, slot]), high, unit
    )

    def whole(piece):
        return lax.all_gather(after(piece, *chunks[1:]), "ctx", axis=0, tiled=True).astype(F32)

    grad_down = down_whole.astype(F32)
    both = whole(scatter_ctx(part_qo))
    grad_query, grad_output = both[:, :D], both[:, D:]
    rest = whole(scatter_ctx(part_kv))
    pair_both = rest[:, : 2 * KVH * DH].reshape(shard, KVH, 2, DH)
    grad_key = pair_both[:, :, 0].reshape(shard, KVH * DH)
    grad_value = pair_both[:, :, 1].reshape(shard, KVH * DH)
    sums = rest[:, 2 * KVH * DH :]

    return (
        outputs,
        grad_inputs.reshape(micro, local, D),
        sums[:, 0],
        grad_query,
        grad_key,
        grad_value,
        sums[:head_shard, 2],
        sums[:head_shard, 3],
        grad_output,
        sums[:, 1],
        grad_gate,
        grad_up,
        grad_down,
    )


def solution(mesh):
    rows = P(None, ("fsdp", "ctx"), None)
    tree = P(None, "fsdp", None)
    vector = P("fsdp")
    weight = P("fsdp", None)
    in_specs = (
        rows,
        P(None, ("fsdp", "ctx")),
        tree,
        tree,
        vector,
        weight,
        weight,
        weight,
        vector,
        vector,
        weight,
        vector,
        weight,
        weight,
        weight,
        rows,
    )
    out_specs = (
        rows,
        rows,
        vector,
        weight,
        weight,
        weight,
        vector,
        vector,
        weight,
        vector,
        weight,
        weight,
        weight,
    )
    return jax.shard_map(body, mesh=mesh, in_specs=in_specs, out_specs=out_specs, check_vma=False)
```

```python
import functools

import jax
import jax.numpy as jnp
from jax import lax
from jax.experimental import pallas as pl
from jax.experimental.pallas import tpu as pltpu
from jax.sharding import PartitionSpec as P

D = 2048
QH = 16
KVH = 8
DH = 128
FF = 6144
BLK = 128
GROUP = QH // KVH
SCALE = DH ** (-0.5)
LOG2E = 1.4426950408889634

EPS = 1e-06
BASE = 1000000.0
BF = jnp.bfloat16
F32 = jnp.float32
BLOCK = 512
COST = 100.0
LOW = 45.0
VMEM = 60 * 1024 * 1024


def mat(left, right):
    return jnp.dot(left, right, preferred_element_type=F32)


def dot_last(left, right):
    return lax.dot_general(left, right, (((1,), (1,)), ((), ())), preferred_element_type=F32)


def outer(left, right):
    return lax.dot_general(left, right, (((0,), (0,)), ((), ())), preferred_element_type=F32)


def after(value, *others):
    return lax.optimization_barrier((value,) + others)[0]


def swap(value, bits):
    count = lax.axis_size("fsdp")
    return lax.ppermute(value, "fsdp", [(i, i ^ bits) for i in range(count)])


def inv_rms(values):
    return lax.rsqrt(jnp.mean(values * values, axis=-1, keepdims=True) + EPS)


def rms_back(values, inv, gain, dy):
    product = dy * values
    dv = inv * (gain * dy) - values * (inv * inv * inv) * jnp.mean(
        product * gain, axis=-1, keepdims=True
    )
    return dv, jnp.sum(product * inv, axis=0)


def call(
    kernel,
    name,
    grid,
    in_specs,
    out_specs,
    out_shape,
    flops,
    moved,
    scratch=(),
    aliases=None,
    scalars=0,
    cost=COST,
):
    return pl.pallas_call(
        kernel,
        name=name,
        grid_spec=pltpu.PrefetchScalarGridSpec(
            num_scalar_prefetch=scalars,
            grid=grid,
            in_specs=in_specs,
            out_specs=out_specs,
            scratch_shapes=list(scratch),
        ),
        out_shape=out_shape,
        input_output_aliases=aliases or {},
        compiler_params=pltpu.CompilerParams(vmem_limit_bytes=VMEM),
        cost_estimate=pl.CostEstimate(
            flops=int(flops * cost), bytes_accessed=int(moved * cost), transcendentals=0
        ),
    )


def fixed(shape):
    return pl.BlockSpec(
        shape, lambda *index: tuple(0 for _ in shape), pipeline_mode=pl.Buffered(1)
    )


def project(x, weight, first, cols, cosine, sine, gain, kinds, name, cost=COST):
    rows, depth = x.shape
    width = DH * len(kinds)

    def kernel(x_ref, w_ref, c_ref, s_ref, g_ref, out_ref, raw_ref):
        raw = mat(x_ref[...], w_ref[...])
        raw_ref[...] = raw.astype(BF)
        for index, kind in enumerate(kinds):
            part = raw[:, index * DH : (index + 1) * DH]
            if kind == "r":
                part = part * inv_rms(part) * g_ref[...]
                part = part * c_ref[...] + pltpu.roll(part, DH // 2, 1) * s_ref[...]
            out_ref[:, index * DH : (index + 1) * DH] = part.astype(BF)

    whole = lambda j: (0, 0)
    block = lambda j: (0, j)
    return call(
        kernel,
        name,
        (cols // width,),
        [
            pl.BlockSpec((rows, depth), whole),
            pl.BlockSpec((depth, width), lambda j: (0, j + first // width)),
            pl.BlockSpec((rows, DH), whole),
            pl.BlockSpec((rows, DH), whole),
            pl.BlockSpec((1, DH), whole),
        ],
        [pl.BlockSpec((rows, width), block)] * 2,
        [jax.ShapeDtypeStruct((rows, cols), BF)] * 2,
        2 * rows * depth * cols,
        2 * (rows * depth + depth * cols + 2 * rows * cols),
        cost=cost,
    )(x, weight, cosine, sine, gain)


def stack_heads(block):
    return jnp.concatenate([block[:, i * DH : (i + 1) * DH] for i in range(GROUP)], axis=0)


def attention(queries, pairs, mask):
    rows = queries.shape[0]
    keys = pairs.shape[0]

    def kernel(q_ref, kv_ref, m_ref, out_ref, inv_ref):
        stacked = stack_heads(q_ref[...])
        scores = dot_last(kv_ref[:, :DH], stacked)
        mask_now = jnp.concatenate([m_ref[...]] * GROUP, axis=1)
        powers = jnp.exp2(scores * (SCALE * LOG2E)) * mask_now
        inv = 1.0 / jnp.sum(powers, axis=0, keepdims=True)
        inv_ref[0] = inv
        out = (outer(kv_ref[:, DH:], powers.astype(BF)) * inv).T
        for index in range(GROUP):
            out_ref[:, index * DH : (index + 1) * DH] = out[
                index * rows : (index + 1) * rows
            ].astype(BF)

    return call(
        kernel,
        "attention",
        (KVH,),
        [
            pl.BlockSpec((rows, GROUP * DH), lambda g: (0, g)),
            pl.BlockSpec((keys, 2 * DH), lambda g: (0, g)),
            pl.BlockSpec((keys, rows), lambda g: (0, 0)),
        ],
        [
            pl.BlockSpec((rows, GROUP * DH), lambda g: (0, g)),
            pl.BlockSpec((1, 1, GROUP * rows), lambda g: (g, 0, 0)),
        ],
        [
            jax.ShapeDtypeStruct((rows, QH * DH), BF),
            jax.ShapeDtypeStruct((KVH, 1, GROUP * rows), F32),
        ],
        4 * QH * rows * keys * DH,
        2 * (2 * rows * QH * DH + 2 * keys * KVH * DH),
    )(queries, pairs, mask)


def head_back(dy, raw, cosine, sine, gain):
    turned = dy * cosine - pltpu.roll(dy, DH // 2, 1) * sine
    inv = inv_rms(raw)
    product = turned * raw
    dv = inv * (gain * turned) - raw * (inv * inv * inv) * jnp.mean(
        product * gain, axis=-1, keepdims=True
    )
    return dv, jnp.sum(product * inv, axis=0, keepdims=True)


def attention_back(queries, raw, pairs, mask, d_out, out, inv, cosine, sine, gain):
    rows = queries.shape[0]
    keys = pairs.shape[0]

    def kernel(
        q_ref, r_ref, kv_ref, m_ref, do_ref, o_ref, inv_ref, c_ref, s_ref, g_ref,
        dq_ref, dkv_ref, dg_ref,
    ):
        stacked = stack_heads(q_ref[...])
        d_stacked = stack_heads(do_ref[...])
        o_stacked = stack_heads(o_ref[...])
        dots = jnp.sum((d_stacked.astype(F32) * o_stacked.astype(F32)).T, axis=0, keepdims=True)
        scores = dot_last(kv_ref[:, :DH], stacked)
        mask_now = jnp.concatenate([m_ref[...]] * GROUP, axis=1)
        probs = jnp.exp2(scores * (SCALE * LOG2E)) * (mask_now * inv_ref[0])
        d_probs = dot_last(kv_ref[:, DH:], d_stacked)
        d_scores = (probs * (d_probs - dots)).astype(BF)
        dkv_ref[:, DH:] = mat(probs.astype(BF), d_stacked).astype(BF)
        dkv_ref[:, :DH] = (mat(d_scores, stacked) * SCALE).astype(BF)
        d_query = outer(d_scores, kv_ref[:, :DH]) * SCALE
        total = jnp.zeros((1, DH), F32)
        for index in range(GROUP):
            part = slice(index * DH, (index + 1) * DH)
            dv, dg = head_back(
                d_query[index * rows : (index + 1) * rows],
                r_ref[:, part].astype(F32),
                c_ref[...],
                s_ref[...],
                g_ref[...],
            )
            dq_ref[:, part] = dv.astype(BF)
            total = total + dg

        @pl.when(pl.program_id(0) == 0)
        def _():
            dg_ref[...] = jnp.zeros_like(dg_ref)

        dg_ref[...] += total

    head = pl.BlockSpec((rows, GROUP * DH), lambda g: (0, g))
    pair = pl.BlockSpec((keys, 2 * DH), lambda g: (0, g))
    whole = lambda shape: pl.BlockSpec(shape, lambda g: (0, 0))
    return call(
        kernel,
        "attention_back",
        (KVH,),
        [
            head,
            head,
            pair,
            whole((keys, rows)),
            head,
            head,
            pl.BlockSpec((1, 1, GROUP * rows), lambda g: (g, 0, 0)),
            whole((rows, DH)),
            whole((rows, DH)),
            whole((1, DH)),
        ],
        [head, pair, whole((1, DH))],
        [
            jax.ShapeDtypeStruct((rows, QH * DH), BF),
            jax.ShapeDtypeStruct((keys, 2 * KVH * DH), BF),
            jax.ShapeDtypeStruct((1, DH), F32),
        ],
        10 * QH * rows * keys * DH,
        2 * (5 * rows * QH * DH + 4 * keys * KVH * DH),
    )(queries, raw, pairs, mask, d_out, out, inv, cosine, sine, gain)


def pair_back(d_pairs, raw, cosine, sine, gain):
    rows, cols = d_pairs.shape

    def kernel(d_ref, r_ref, c_ref, s_ref, g_ref, out_ref, dg_ref):
        total = jnp.zeros((1, DH), F32)
        for index in range(BLOCK // (2 * DH)):
            part = slice(index * 2 * DH, index * 2 * DH + DH)
            rest = slice(index * 2 * DH + DH, (index + 1) * 2 * DH)
            dv, dg = head_back(
                d_ref[:, part].astype(F32),
                r_ref[:, part].astype(F32),
                c_ref[...],
                s_ref[...],
                g_ref[...],
            )
            out_ref[:, part] = dv.astype(BF)
            out_ref[:, rest] = d_ref[:, rest]
            total = total + dg

        @pl.when(pl.program_id(0) == 0)
        def _():
            dg_ref[...] = jnp.zeros_like(dg_ref)

        dg_ref[...] += total

    block = pl.BlockSpec((rows, BLOCK), lambda j: (0, j))
    whole = lambda shape: pl.BlockSpec(shape, lambda j: (0, 0))
    return call(
        kernel,
        "pair_back",
        (cols // BLOCK,),
        [block, block, whole((rows, DH)), whole((rows, DH)), whole((1, DH))],
        [block, whole((1, DH))],
        [jax.ShapeDtypeStruct((rows, cols), BF), jax.ShapeDtypeStruct((1, DH), F32)],
        20 * rows * cols,
        6 * rows * cols,
        cost=LOW,
    )(d_pairs, raw, cosine, sine, gain)


def feed(mids, cots, pieces, w_down, index, total, earlier, place):
    rows, depth = mids[0].shape
    parts = len(mids)
    hidden = w_down.shape[0]
    count = len(pieces)
    unit = place[1]
    steps = hidden // unit
    block_rows = depth // (4 * count)

    def kernel(me_ref, *refs):
        mid_refs = refs[:parts]
        cot_refs = refs[parts : 2 * parts]
        piece_refs = refs[2 * parts : 2 * parts + count]
        wd_ref = refs[2 * parts + count]
        if count > 1:
            act_ref, d_ref, wp_ref = refs[-3:]
            for which in range(4 * count):
                start = pl.multiple_of((me_ref[0] ^ which) * block_rows, block_rows)
                near = which % 4 * block_rows
                wp_ref[pl.ds(start, block_rows), :] = piece_refs[which // 4][
                    near : near + block_rows
                ]
        else:
            act_ref, d_ref = refs[-2:]
            wp_ref = piece_refs[0]
        for part in range(parts):
            now = slice(part * rows, (part + 1) * rows)
            both = mat(mid_refs[part][...], wp_ref[...])
            gate = both[:, :unit]
            up = both[:, unit:]
            d_act = dot_last(cot_refs[part][...], wd_ref[...])
            sig = 1.0 / (1.0 + jnp.exp2(gate * (-LOG2E)))
            silu = gate * sig
            act_ref[now] = (silu * up).astype(BF)
            d_ref[now, unit:] = (d_act * silu).astype(BF)
            d_ref[now, :unit] = (d_act * up * (sig + silu * (1.0 - sig))).astype(BF)

    def piece_spec(far):
        return pl.BlockSpec((pieces[0].shape[0], 2 * unit), lambda j, me: (0, j ^ far))

    out_specs = [
        pl.BlockSpec((parts * rows, unit), lambda j, me: (index, j)),
        pl.BlockSpec((parts * rows, 2 * unit), lambda j, me: (index, j)),
    ]
    out_shape = [
        jax.ShapeDtypeStruct((total * parts * rows, hidden), BF),
        jax.ShapeDtypeStruct((total * parts * rows, 2 * hidden), BF),
    ]
    if count > 1:
        out_specs.append(pl.BlockSpec((depth, 2 * unit), lambda j, me: (0, j)))
        out_shape.append(jax.ShapeDtypeStruct((depth, 2 * hidden), BF))
    before = 1 + 2 * parts + count + 1
    return call(
        kernel,
        "feed",
        (steps,),
        [fixed((rows, depth))] * parts
        + [
            pl.BlockSpec(
                (rows, depth), lambda j, me: (index, 0), pipeline_mode=pl.Buffered(1)
            )
        ]
        * parts
        + [piece_spec(which) for which in range(count)]
        + [pl.BlockSpec((unit, depth), lambda j, me: (j, 0))]
        + [pl.BlockSpec(memory_space=pl.ANY)] * len(earlier),
        out_specs,
        out_shape,
        6 * parts * rows * depth * hidden,
        2 * (2 * parts * rows * depth + 3 * depth * hidden + 3 * parts * rows * hidden),
        aliases={before + i: i for i in range(len(earlier))},
        scalars=1,
    )(place[0], *mids, *cots, *pieces, w_down, *earlier)


def feed_out(left, weight, index, parts, transposed, name, dtype=BF):
    depth = left.shape[1]
    cols = weight.shape[0] if transposed else weight.shape[1]
    rows = parts[1]

    def kernel(a_ref, w_ref, *outs):
        for part in range(parts[0]):
            now = a_ref[part * rows : (part + 1) * rows]
            result = dot_last(now, w_ref[...]) if transposed else mat(now, w_ref[...])
            outs[part][...] = result.astype(dtype)

    return call(
        kernel,
        name,
        (cols // BLOCK,),
        [
            pl.BlockSpec((parts[0] * rows, depth), lambda j: (index, 0)),
            pl.BlockSpec((BLOCK, depth), lambda j: (j, 0))
            if transposed
            else pl.BlockSpec((depth, BLOCK), lambda j: (0, j)),
        ],
        [pl.BlockSpec((rows, BLOCK), lambda j: (0, j))] * parts[0],
        [jax.ShapeDtypeStruct((rows, cols), dtype)] * parts[0],
        2 * parts[0] * rows * depth * cols,
        2 * (parts[0] * rows * (depth + cols) + depth * cols),
    )(left, weight)


def weight_terms(lefts, block, starts, width, size, rights, step, added, chunked, name, turn=0, cost=COST):
    depth = sum(left.shape[0] for left in lefts)
    cols = rights[0][0].shape[1]
    size_right = depth // len(rights)
    blocks = starts.shape[0]
    rows = blocks * size
    steps = cols // step
    nl, nr = len(lefts), len(rights)

    def kernel(block_ref, start_ref, *refs):
        left_refs = refs[:nl]
        right_refs = refs[nl : nl + nr]
        add_refs = refs[nl + nr : nl + nr + len(added)]
        out_ref, turned = refs[-2:]

        @pl.when(pl.program_id(0) == 0)
        def _():
            for which in range(blocks):
                start = pl.multiple_of(start_ref[which], 128)
                at = 0
                for ref in left_refs:
                    turned[which * size : (which + 1) * size, at : at + ref.shape[0]] = ref[
                        :, pl.ds(start, size)
                    ].T
                    at += ref.shape[0]

        right = [ref[...] for ref in right_refs]
        right = right[0] if nr == 1 else jnp.concatenate(right, axis=0)
        result = mat(turned[...], right)
        for ref in add_refs:
            result = result + ref[...].astype(F32)
        out_ref[...] = result.astype(BF)

    if chunked:
        out_spec = pl.BlockSpec((rows, step), lambda j, b, s: (j ^ turn, 0))
        shape = (steps * rows, step)
    else:
        out_spec = pl.BlockSpec((rows, step), lambda j, b, s: (0, j))
        shape = (rows, cols)
    return call(
        kernel,
        name,
        (steps,),
        [
            pl.BlockSpec(
                (left.shape[0], width), lambda j, b, s: (0, b[0]), pipeline_mode=pl.Buffered(1)
            )
            for left in lefts
        ]
        + [
            pl.BlockSpec((size_right, step), functools.partial(lambda at, j, b, s: (at, j), at))
            for right, at in rights
        ]
        + [out_spec] * len(added),
        out_spec,
        jax.ShapeDtypeStruct(shape, BF),
        2 * rows * depth * cols,
        2 * (rows * depth + depth * cols + (1 + len(added)) * rows * cols),
        scratch=[pltpu.VMEM((rows, depth), BF)],
        scalars=2,
        cost=cost,
    )(block, starts, *lefts, *[right for right, at in rights], *added)


def column_parts(gate, up, high, slots, number):
    rows, cols = gate.shape
    unit = cols // (4 * high)

    def kernel(slot_ref, gate_ref, up_ref, out_ref):
        out_ref[:, :unit] = gate_ref[...]
        out_ref[:, unit:] = up_ref[...]

    block = pl.BlockSpec((rows, unit), lambda i, j, at: (0, (at[0] ^ j) * 4 + at[i + 1]))
    return call(
        kernel,
        "column_parts",
        (number, high),
        [block, block],
        pl.BlockSpec((rows, 2 * unit), lambda i, j, at: (i, j)),
        jax.ShapeDtypeStruct((number * rows, 2 * unit * high), BF),
        0,
        8 * number * rows * unit * high,
        scalars=1,
    )(slots, gate, up)


def lay_pairs(chunks, place, high, unit):
    depth = chunks.shape[0] // 4
    rows = chunks.shape[1]
    cols = 4 * high * unit
    size = rows // 4

    def kernel(place_ref, *refs):
        for which in range(depth):
            out_ref = refs[depth + which % 2]
            far = place_ref[0] ^ (which // 2)
            for near in range(4):
                start = pl.multiple_of((far * 4 + (place_ref[1] ^ near)) * unit, 128)
                out_ref[:, pl.ds(start, unit)] = refs[which][near].astype(F32)

    return call(
        kernel,
        "lay_pairs",
        (4,),
        [
            pl.BlockSpec((4, size, unit), functools.partial(lambda w, i, at: (w, i, 0), which))
            for which in range(depth)
        ],
        [pl.BlockSpec((size, cols), lambda i, at: (i, 0))] * 2,
        [jax.ShapeDtypeStruct((rows, cols), F32)] * 2,
        0,
        12 * rows * cols,
        scalars=1,
    )(place, *[chunks] * depth)


def visibility(parent, layout, offset, count):
    blocks = parent.shape[0]
    ident = jnp.arange(blocks, dtype=jnp.int32)
    current = ident
    reach = ident[:, None] == ident[None, :]
    for step in range(blocks):
        current = jnp.sum(jnp.where(current[:, None] == ident[None, :], parent[None, :], 0), axis=1)
        reach = reach | (current[:, None] == ident[None, :])
    place = (layout[:, None] == ident[None, :]).astype(jnp.int32)
    picked = jnp.sum(place[:, :, None] * reach.astype(jnp.int32)[None, :, :], axis=1)
    row_reach = jnp.sum(picked[:, None, :] * place[None, :, :], axis=2) > 0
    mine = lax.dynamic_slice_in_dim(row_reach, offset // BLK, count // BLK, 0).T
    spread = jnp.broadcast_to(
        mine[:, None, :, None], (blocks, BLK, count // BLK, BLK)
    ).reshape(blocks * BLK, count)
    query_rows = offset + lax.broadcasted_iota(jnp.int32, (blocks * BLK, count), 1)
    key_rows = lax.broadcasted_iota(jnp.int32, (blocks * BLK, count), 0)
    same = query_rows // BLK == key_rows // BLK
    return (spread & (jnp.logical_not(same) | (key_rows <= query_rows))).astype(F32)


def gather_small(vector, me):
    count = lax.axis_size("fsdp")
    buffer = jnp.zeros((count,) + vector.shape, vector.dtype)
    buffer = lax.dynamic_update_index_in_dim(buffer, vector, me, 0)
    step = 1
    while step < count:
        buffer = buffer + swap(buffer, step)
        step *= 2
    return buffer


def gather_rows(shard):
    high = lax.axis_size("fsdp") // 4
    return jnp.concatenate(
        [shard] + [swap(shard, 4 * far) for far in range(1, high)], axis=0
    )


def group_rows(rows):
    from_x = swap(rows, 2)
    from_core = swap(rows, 1)
    from_both = swap(from_x, 1)
    return [rows, from_core, from_x, from_both]


def group_half(parts):
    got = swap(jnp.concatenate([parts[1], parts[3]], axis=0), 1)
    rows = parts[0].shape[0]
    own = parts[0].astype(F32) + got[:rows].astype(F32)
    return own, (parts[2].astype(F32) + got[rows:].astype(F32)).astype(BF)


def scatter_ctx(array):
    return lax.psum_scatter(array, "ctx", scatter_dimension=0, tiled=True)


def spread_near(piece, me):
    slot = me % 4
    rows = piece.shape[0] // 4
    near = [lax.dynamic_slice_in_dim(piece, (slot ^ which) * rows, rows, 0) for which in range(4)]
    return near, jnp.stack([near[0]] + [swap(near[which], which) for which in range(1, 4)])


def fold(value, bits, *others):
    for bit in bits:
        half = value.shape[0] // 2
        got = swap(value[half:], bit)
        keep = after(value[:half], *others) if others else value[:half]
        value = (keep.astype(F32) + got.astype(F32)).astype(BF)
        others = ()
    return value


def order_of(bits):
    order = [0]
    for bit in reversed(bits):
        order = order + [entry ^ bit for entry in order]
    return order


def body(
    inputs,
    depths,
    parents,
    layout,
    gain_attn,
    w_query,
    w_key,
    w_value,
    query_gain,
    key_gain,
    w_output,
    gain_ffn,
    w_gate,
    w_up,
    w_down,
    cotangent,
):
    me = lax.axis_index("fsdp")
    micro, local, _ = inputs.shape
    total = micro * local
    offset = lax.axis_index("ctx") * local
    count = lax.axis_size("fsdp")
    shard = D // count
    head_shard = DH // count

    def rows_of(index):
        return slice(index * local, (index + 1) * local)

    pair_shard = jnp.stack(
        [w_key.reshape(shard, KVH, DH), w_value.reshape(shard, KVH, DH)], axis=2
    ).reshape(shard, 2 * KVH * DH)
    gains = gather_small(jnp.concatenate([gain_attn, gain_ffn, query_gain, key_gain]), me)
    w_qkv = lax.all_gather(
        jnp.concatenate([w_query, pair_shard], axis=1), "fsdp", axis=0, tiled=True
    )
    attn_gain = gains[:, :shard].reshape(D).astype(F32)
    ffn_gain = gains[:, shard : 2 * shard].reshape(D).astype(F32)
    q_gain = gains[:, 2 * shard : 2 * shard + head_shard].reshape(1, DH).astype(F32)
    k_gain = gains[:, 2 * shard + head_shard :].reshape(1, DH).astype(F32)

    unit = FF // count
    high = count // 4
    slot = me % 4
    parts_x = column_parts(w_gate, w_up, high, jnp.stack([me // 4, slot ^ 2, slot ^ 3]), 2)
    parts_own = column_parts(
        after(w_gate, parts_x), w_up, high, jnp.stack([me // 4, slot, slot ^ 1]), 2
    )
    got_x = swap(after(parts_x, w_qkv, gains), 2)
    wd = gather_rows(after(w_down, w_qkv, gains))
    out_pieces = [w_output]
    out_order = [0]
    bit = count // 2
    while bit > 2:
        out_pieces += [swap(piece, bit) for piece in out_pieces]
        out_order += [entry ^ bit for entry in out_order]
        bit //= 2
    out_block = jnp.concatenate(out_pieces, axis=0)
    cot_all = cotangent.reshape(total, D)

    freq = jnp.power(BASE, -jnp.arange(DH // 2, dtype=F32) / (DH // 2))
    angle = depths.reshape(total).astype(F32)[:, None] * freq[None, :]
    cosine = jnp.cos(angle)
    sine = jnp.sin(angle)
    cosine = jnp.concatenate([cosine, cosine], axis=1)
    sine = jnp.concatenate([-sine, sine], axis=1)
    masks = [
        visibility(parents[index, 0], layout[index, 0], offset, local) for index in range(micro)
    ]

    source = inputs.reshape(total, D).astype(F32)
    inv_in = inv_rms(source)
    normed_b = (source * inv_in * attn_gain).astype(BF)
    normed_now = after(normed_b, parts_own, out_block, *masks)
    pairs, pairs_raw = project(
        normed_now,
        w_qkv,
        QH * DH,
        2 * KVH * DH,
        cosine,
        sine,
        k_gain,
        "r-r-",
        "project_pairs",
    )
    everyone = [
        lax.all_gather(pairs[rows_of(index)], "ctx", axis=0, tiled=True) for index in range(micro)
    ]
    got_core = swap(
        jnp.concatenate([parts_own[shard:], after(got_x, pairs, wd)[shard:]], axis=0), 1
    )
    near = jnp.concatenate(
        [parts_own[:shard], got_core[:shard], got_x[:shard], got_core[shard:]], axis=0
    )
    queries, queries_raw = project(
        after(normed_b, pairs, near, wd),
        w_qkv,
        0,
        QH * DH,
        cosine,
        sine,
        q_gain,
        "rrrr",
        "project_queries",
        0.01,
    )
    pieces = [near] + [swap(near, 4 * far) for far in range(1, high)]
    for bit, earlier in ((2, near), (1, everyone[0])):
        out_block = jnp.concatenate([out_block, swap(after(out_block, earlier), bit)], axis=0)
        out_order = out_order + [entry ^ bit for entry in out_order]
    w_out = jnp.zeros((QH * DH, D), BF)
    for index, entry in enumerate(out_order):
        w_out = lax.dynamic_update_slice_in_dim(
            w_out, out_block[index * shard : (index + 1) * shard], (me ^ entry) * shard, 0
        )
    cot_x = swap(after(cot_all, near), 2)
    cot_rows = [cot_all, swap(cot_all, 1), cot_x, swap(cot_x, 1)]

    attended = []
    inverses = []
    middles = []
    mid_inverses = []
    mid_rows = []
    token = queries
    for index in range(micro):
        part = rows_of(index)
        if index == 0:
            token = (token,)
        else:
            token = (token, cot_x)
        out, inverse = attention(after(queries[part], *token), everyone[index], masks[index])
        middle = source[part] + mat(after(out, w_out) if index == 0 else out, w_out)
        inv_mid = inv_rms(middle)
        mid_b = (middle * inv_mid * ffn_gain).astype(BF)
        attended.append(out)
        inverses.append(inverse)
        middles.append(middle)
        mid_inverses.append(inv_mid)
        mid_rows.append(group_rows(mid_b))
        token = mid_b

    mid_pieces = [piece for rows in mid_rows for piece in rows]
    cot_pieces = [(piece, index) for index in range(micro) for piece in cot_rows]
    zero = jnp.zeros((1,), jnp.int32)

    def down_terms(act, far, added, cost=COST):
        return weight_terms(
            [act],
            zero + far,
            zero,
            unit,
            unit,
            cot_pieces,
            BLOCK,
            added,
            False,
            "grad_down",
            cost=cost,
        )

    def pair_terms(first, far, added, cost=COST):
        return weight_terms(
            [first] + mid_pieces[1:],
            ((me // 4) ^ far)[None],
            zero,
            D // high,
            D // high,
            [(dgu_b, 0)],
            unit,
            added,
            True,
            "grad_pair",
            2 * far,
            cost,
        )

    d_mids = []
    me_array = me[None]
    act_b, dgu_b, wgu = feed(
        [after(mid_rows[0][0], token)] + mid_rows[0][1:],
        cot_rows,
        pieces,
        wd,
        0,
        micro,
        (),
        (me_array, unit),
    )
    def send_back(index, token):
        parts = feed_out(
            after(dgu_b, token), wgu, index, (4, local), True, "feed_back"
        )
        d_mids.append(group_half(parts))
        return parts[0]

    d_middles = []
    d_projs = []
    d_query_parts = []
    d_pair_parts = []
    d_ffn_gain = jnp.zeros((D,), F32)
    d_q_gain = jnp.zeros((1, DH), F32)
    token = act_b
    for index in range(1, micro):
        token = send_back(index - 1, token)
        act_b, dgu_b = feed(
            [after(mid_rows[index][0], token, d_mids[index - 1][1])] + mid_rows[index][1:],
            cot_rows,
            [wgu],
            wd,
            index,
            micro,
            (act_b, dgu_b),
            (me_array, unit),
        )
        token = act_b
    sent_pair = []
    sent_down = []
    for far in range(1, high):
        sent_pair.append(pair_terms(after(mid_pieces[0], token), far, []))
        token = sent_pair[-1]
    got_pair = [swap(piece, 4 * (far + 1)) for far, piece in enumerate(sent_pair)]
    for index in range(micro):
        part = rows_of(index)
        if index == micro - 1:
            token = send_back(index, token)
            for far in range(1, high):
                sent_down.append(down_terms(after(act_b, token, d_mids[index][1]), far, []))
                token = sent_down[-1]
            got_down = [swap(piece, 4 * (far + 1)) for far, piece in enumerate(sent_down)]
        d_mid = d_mids[index][0] + swap(d_mids[index][1], 2).astype(F32)
        d_part, d_gain = rms_back(
            middles[index], mid_inverses[index], ffn_gain, after(d_mid, token)
        )
        d_ffn_gain = d_ffn_gain + d_gain
        d_middle = cotangent[index].astype(F32) + d_part
        d_proj = d_middle.astype(BF)
        d_attended = dot_last(d_proj, w_out).astype(BF)
        d_query, d_pair, d_gain = attention_back(
            queries[part],
            queries_raw[part],
            everyone[index],
            masks[index],
            d_attended,
            attended[index],
            inverses[index],
            cosine[part],
            sine[part],
            q_gain,
        )
        d_q_gain = d_q_gain + d_gain
        d_middles.append(d_middle)
        d_projs.append(d_proj)
        d_query_parts.append(d_query)
        d_pair_parts.append(scatter_ctx(d_pair))
        token = d_query

    d_query_b = jnp.concatenate(d_query_parts, axis=0)
    d_proj_b = jnp.concatenate(d_projs, axis=0)
    attended_b = jnp.concatenate(attended, axis=0)
    bits = [2**i for i in range(count.bit_length() - 1)]
    half_size = count // 2

    def plain_terms(left, right, order, added, name, cost=COST):
        starts = (me ^ jnp.array(order, jnp.int32)) * shard
        return weight_terms(
            [left], zero, starts, D, shard, [(right, 0)], BLOCK, added, False, name, cost=cost
        )

    order = order_of(bits)
    out_parts = []
    for index in range(micro):
        out_parts.append(
            feed_out(after(act_b, token), wd, index, (4, local), False, "feed_forward")
        )
        token = out_parts[-1][0]
    out_half = group_half([jnp.concatenate(list(pair), axis=0) for pair in zip(*out_parts)])
    sent_query = plain_terms(after(normed_b, token), d_query_b, order[half_size:], [], "grad_q")
    sent_output = plain_terms(
        after(attended_b, sent_query), d_proj_b, order[half_size:], [], "grad_o"
    )
    own_pair = pair_terms(after(mid_pieces[0], sent_output, out_half[1]), 0, got_pair)
    own_query = plain_terms(
        after(normed_b, own_pair), d_query_b, order[:half_size], [swap(sent_query, 1)], "grad_q"
    )
    own_output = plain_terms(
        after(attended_b, own_query), d_proj_b, order[:half_size], [swap(sent_output, 1)], "grad_o"
    )
    own_down = down_terms(after(act_b, own_output), 0, got_down)
    outputs = jnp.concatenate(middles, axis=0) + out_half[0]
    outputs = (outputs + swap(out_half[1], 2).astype(F32)).astype(BF).reshape(micro, local, D)
    pair_piece = scatter_ctx(own_pair)
    down_piece = scatter_ctx(after(own_down, own_pair))

    d_pairs = after(jnp.concatenate(d_pair_parts, axis=0), own_down, outputs)
    d_pair_b, d_k_gain = pair_back(d_pairs, pairs_raw, cosine, sine, k_gain)
    part_qo = [fold(own_query, bits[1:2], d_pair_b), fold(own_output, bits[1:2], d_pair_b)]
    sent_kv = plain_terms(after(normed_b, *part_qo), d_pair_b, order[half_size:], [], "grad_kv", LOW)
    (d_normed,) = feed_out(
        jnp.concatenate([after(d_query_b, sent_kv), d_pair_b], axis=1),
        w_qkv,
        0,
        (1, total),
        True,
        "d_normed",
        F32,
    )
    own_kv = plain_terms(
        after(normed_b, d_normed), d_pair_b, order[:half_size], [swap(sent_kv, 1)], "grad_kv"
    )
    d_source, d_attn_gain = rms_back(source, inv_in, attn_gain, after(d_normed, own_kv))
    grad_inputs = jnp.concatenate(d_middles, axis=0) + d_source

    def spread(vector):
        return jnp.pad(vector.reshape(count, -1), ((0, 0), (0, shard - vector.size // count)))

    columns = jnp.stack(
        [
            d_attn_gain.reshape(count, shard),
            d_ffn_gain.reshape(count, shard),
            spread(d_q_gain),
            spread(d_k_gain),
        ],
        axis=2,
    ).astype(BF)
    columns = jnp.pad(columns, ((0, 0), (0, 0), (0, DH - 4))).reshape(D, DH)
    columns = jnp.concatenate(
        [
            lax.dynamic_slice_in_dim(columns, (me ^ entry) * shard, shard, 0)
            for entry in order
        ],
        axis=0,
    )
    columns = fold(columns, bits[:1])
    near_parts, pair_near = spread_near(pair_piece, me)
    chunks = lax.all_gather(pair_near, "ctx", axis=0, tiled=True)
    down_whole = lax.all_gather(down_piece, "ctx", axis=0, tiled=True)
    part_qo = fold(jnp.concatenate(part_qo, axis=1), bits[2:])
    part_kv = fold(
        jnp.concatenate([after(own_kv, *near_parts), columns], axis=1), bits[1:2], pair_near
    )
    part_kv = fold(part_kv, bits[2:])

    grad_gate, grad_up = lay_pairs(
        chunks, jnp.stack([me // 4, slot]), high, unit
    )

    def whole(piece):
        return lax.all_gather(piece, "ctx", axis=0, tiled=True).astype(F32)

    grad_down = down_whole.astype(F32)
    both = whole(scatter_ctx(part_qo))
    grad_query, grad_output = both[:, :D], both[:, D:]
    rest = whole(scatter_ctx(part_kv))
    pair_both = rest[:, : 2 * KVH * DH].reshape(shard, KVH, 2, DH)
    grad_key = pair_both[:, :, 0].reshape(shard, KVH * DH)
    grad_value = pair_both[:, :, 1].reshape(shard, KVH * DH)
    sums = rest[:, 2 * KVH * DH :]

    return (
        outputs,
        grad_inputs.reshape(micro, local, D),
        sums[:, 0],
        grad_query,
        grad_key,
        grad_value,
        sums[:head_shard, 2],
        sums[:head_shard, 3],
        grad_output,
        sums[:, 1],
        grad_gate,
        grad_up,
        grad_down,
    )


def solution(mesh):
    rows = P(None, ("fsdp", "ctx"), None)
    tree = P(None, "fsdp", None)
    vector = P("fsdp")
    weight = P("fsdp", None)
    in_specs = (
        rows,
        P(None, ("fsdp", "ctx")),
        tree,
        tree,
        vector,
        weight,
        weight,
        weight,
        vector,
        vector,
        weight,
        vector,
        weight,
        weight,
        weight,
        rows,
    )
    out_specs = (
        rows,
        rows,
        vector,
        weight,
        weight,
        weight,
        vector,
        vector,
        weight,
        vector,
        weight,
        weight,
        weight,
    )
    return jax.shard_map(body, mesh=mesh, in_specs=in_specs, out_specs=out_specs, check_vma=False)
```

```python
import functools

import jax
import jax.numpy as jnp
from jax import lax
from jax.experimental import pallas as pl
from jax.experimental.pallas import tpu as pltpu
from jax.sharding import PartitionSpec as P

D = 2048
QH = 16
KVH = 8
DH = 128
FF = 6144
BLK = 128
GROUP = QH // KVH
SCALE = DH ** (-0.5)
LOG2E = 1.4426950408889634

EPS = 1e-06
BASE = 1000000.0
BF = jnp.bfloat16
F32 = jnp.float32
BLOCK = 512
COST = 100.0
LOW = 45.0
VMEM = 60 * 1024 * 1024


def mat(left, right):
    return jnp.dot(left, right, preferred_element_type=F32)


def dot_last(left, right):
    return lax.dot_general(left, right, (((1,), (1,)), ((), ())), preferred_element_type=F32)


def outer(left, right):
    return lax.dot_general(left, right, (((0,), (0,)), ((), ())), preferred_element_type=F32)


def after(value, *others):
    return lax.optimization_barrier((value,) + others)[0]


def swap(value, bits):
    count = lax.axis_size("fsdp")
    return lax.ppermute(value, "fsdp", [(i, i ^ bits) for i in range(count)])


def inv_rms(values):
    return lax.rsqrt(jnp.mean(values * values, axis=-1, keepdims=True) + EPS)


def rms_back(values, inv, gain, dy):
    product = dy * values
    dv = inv * (gain * dy) - values * (inv * inv * inv) * jnp.mean(
        product * gain, axis=-1, keepdims=True
    )
    return dv, jnp.sum(product * inv, axis=0)


def call(
    kernel,
    name,
    grid,
    in_specs,
    out_specs,
    out_shape,
    flops,
    moved,
    scratch=(),
    aliases=None,
    scalars=0,
    cost=COST,
):
    return pl.pallas_call(
        kernel,
        name=name,
        grid_spec=pltpu.PrefetchScalarGridSpec(
            num_scalar_prefetch=scalars,
            grid=grid,
            in_specs=in_specs,
            out_specs=out_specs,
            scratch_shapes=list(scratch),
        ),
        out_shape=out_shape,
        input_output_aliases=aliases or {},
        compiler_params=pltpu.CompilerParams(vmem_limit_bytes=VMEM),
        cost_estimate=pl.CostEstimate(
            flops=int(flops * cost), bytes_accessed=int(moved * cost), transcendentals=0
        ),
    )


def fixed(shape):
    return pl.BlockSpec(
        shape, lambda *index: tuple(0 for _ in shape), pipeline_mode=pl.Buffered(1)
    )


def project(x, weight, first, cols, cosine, sine, gain, kinds, name, cost=COST):
    rows, depth = x.shape
    width = DH * len(kinds)

    def kernel(x_ref, w_ref, c_ref, s_ref, g_ref, out_ref, raw_ref):
        raw = mat(x_ref[...], w_ref[...])
        raw_ref[...] = raw.astype(BF)
        for index, kind in enumerate(kinds):
            part = raw[:, index * DH : (index + 1) * DH]
            if kind == "r":
                part = part * inv_rms(part) * g_ref[...]
                part = part * c_ref[...] + pltpu.roll(part, DH // 2, 1) * s_ref[...]
            out_ref[:, index * DH : (index + 1) * DH] = part.astype(BF)

    whole = lambda j: (0, 0)
    block = lambda j: (0, j)
    return call(
        kernel,
        name,
        (cols // width,),
        [
            pl.BlockSpec((rows, depth), whole),
            pl.BlockSpec((depth, width), lambda j: (0, j + first // width)),
            pl.BlockSpec((rows, DH), whole),
            pl.BlockSpec((rows, DH), whole),
            pl.BlockSpec((1, DH), whole),
        ],
        [pl.BlockSpec((rows, width), block)] * 2,
        [jax.ShapeDtypeStruct((rows, cols), BF)] * 2,
        2 * rows * depth * cols,
        2 * (rows * depth + depth * cols + 2 * rows * cols),
        cost=cost,
    )(x, weight, cosine, sine, gain)


def stack_heads(block):
    return jnp.concatenate([block[:, i * DH : (i + 1) * DH] for i in range(GROUP)], axis=0)


def attention(queries, pairs, mask):
    rows = queries.shape[0]
    keys = pairs.shape[0]

    def kernel(q_ref, kv_ref, m_ref, out_ref, inv_ref):
        stacked = stack_heads(q_ref[...])
        scores = dot_last(kv_ref[:, :DH], stacked)
        mask_now = jnp.concatenate([m_ref[...]] * GROUP, axis=1)
        powers = jnp.exp2(scores * (SCALE * LOG2E)) * mask_now
        inv = 1.0 / jnp.sum(powers, axis=0, keepdims=True)
        inv_ref[0] = inv
        out = (outer(kv_ref[:, DH:], powers.astype(BF)) * inv).T
        for index in range(GROUP):
            out_ref[:, index * DH : (index + 1) * DH] = out[
                index * rows : (index + 1) * rows
            ].astype(BF)

    return call(
        kernel,
        "attention",
        (KVH,),
        [
            pl.BlockSpec((rows, GROUP * DH), lambda g: (0, g)),
            pl.BlockSpec((keys, 2 * DH), lambda g: (0, g)),
            pl.BlockSpec((keys, rows), lambda g: (0, 0)),
        ],
        [
            pl.BlockSpec((rows, GROUP * DH), lambda g: (0, g)),
            pl.BlockSpec((1, 1, GROUP * rows), lambda g: (g, 0, 0)),
        ],
        [
            jax.ShapeDtypeStruct((rows, QH * DH), BF),
            jax.ShapeDtypeStruct((KVH, 1, GROUP * rows), F32),
        ],
        4 * QH * rows * keys * DH,
        2 * (2 * rows * QH * DH + 2 * keys * KVH * DH),
    )(queries, pairs, mask)


def head_back(dy, raw, cosine, sine, gain):
    turned = dy * cosine - pltpu.roll(dy, DH // 2, 1) * sine
    inv = inv_rms(raw)
    product = turned * raw
    dv = inv * (gain * turned) - raw * (inv * inv * inv) * jnp.mean(
        product * gain, axis=-1, keepdims=True
    )
    return dv, jnp.sum(product * inv, axis=0, keepdims=True)


def attention_back(queries, raw, pairs, mask, d_out, out, inv, cosine, sine, gain):
    rows = queries.shape[0]
    keys = pairs.shape[0]

    def kernel(
        q_ref, r_ref, kv_ref, m_ref, do_ref, o_ref, inv_ref, c_ref, s_ref, g_ref,
        dq_ref, dkv_ref, dg_ref,
    ):
        stacked = stack_heads(q_ref[...])
        d_stacked = stack_heads(do_ref[...])
        o_stacked = stack_heads(o_ref[...])
        dots = jnp.sum((d_stacked.astype(F32) * o_stacked.astype(F32)).T, axis=0, keepdims=True)
        scores = dot_last(kv_ref[:, :DH], stacked)
        mask_now = jnp.concatenate([m_ref[...]] * GROUP, axis=1)
        probs = jnp.exp2(scores * (SCALE * LOG2E)) * (mask_now * inv_ref[0])
        d_probs = dot_last(kv_ref[:, DH:], d_stacked)
        d_scores = (probs * (d_probs - dots)).astype(BF)
        dkv_ref[:, DH:] = mat(probs.astype(BF), d_stacked).astype(BF)
        dkv_ref[:, :DH] = (mat(d_scores, stacked) * SCALE).astype(BF)
        d_query = outer(d_scores, kv_ref[:, :DH]) * SCALE
        total = jnp.zeros((1, DH), F32)
        for index in range(GROUP):
            part = slice(index * DH, (index + 1) * DH)
            dv, dg = head_back(
                d_query[index * rows : (index + 1) * rows],
                r_ref[:, part].astype(F32),
                c_ref[...],
                s_ref[...],
                g_ref[...],
            )
            dq_ref[:, part] = dv.astype(BF)
            total = total + dg

        @pl.when(pl.program_id(0) == 0)
        def _():
            dg_ref[...] = jnp.zeros_like(dg_ref)

        dg_ref[...] += total

    head = pl.BlockSpec((rows, GROUP * DH), lambda g: (0, g))
    pair = pl.BlockSpec((keys, 2 * DH), lambda g: (0, g))
    whole = lambda shape: pl.BlockSpec(shape, lambda g: (0, 0))
    return call(
        kernel,
        "attention_back",
        (KVH,),
        [
            head,
            head,
            pair,
            whole((keys, rows)),
            head,
            head,
            pl.BlockSpec((1, 1, GROUP * rows), lambda g: (g, 0, 0)),
            whole((rows, DH)),
            whole((rows, DH)),
            whole((1, DH)),
        ],
        [head, pair, whole((1, DH))],
        [
            jax.ShapeDtypeStruct((rows, QH * DH), BF),
            jax.ShapeDtypeStruct((keys, 2 * KVH * DH), BF),
            jax.ShapeDtypeStruct((1, DH), F32),
        ],
        10 * QH * rows * keys * DH,
        2 * (5 * rows * QH * DH + 4 * keys * KVH * DH),
    )(queries, raw, pairs, mask, d_out, out, inv, cosine, sine, gain)


def pair_back(d_pairs, raw, cosine, sine, gain):
    rows, cols = d_pairs.shape

    def kernel(d_ref, r_ref, c_ref, s_ref, g_ref, out_ref, dg_ref):
        total = jnp.zeros((1, DH), F32)
        for index in range(BLOCK // (2 * DH)):
            part = slice(index * 2 * DH, index * 2 * DH + DH)
            rest = slice(index * 2 * DH + DH, (index + 1) * 2 * DH)
            dv, dg = head_back(
                d_ref[:, part].astype(F32),
                r_ref[:, part].astype(F32),
                c_ref[...],
                s_ref[...],
                g_ref[...],
            )
            out_ref[:, part] = dv.astype(BF)
            out_ref[:, rest] = d_ref[:, rest]
            total = total + dg

        @pl.when(pl.program_id(0) == 0)
        def _():
            dg_ref[...] = jnp.zeros_like(dg_ref)

        dg_ref[...] += total

    block = pl.BlockSpec((rows, BLOCK), lambda j: (0, j))
    whole = lambda shape: pl.BlockSpec(shape, lambda j: (0, 0))
    return call(
        kernel,
        "pair_back",
        (cols // BLOCK,),
        [block, block, whole((rows, DH)), whole((rows, DH)), whole((1, DH))],
        [block, whole((1, DH))],
        [jax.ShapeDtypeStruct((rows, cols), BF), jax.ShapeDtypeStruct((1, DH), F32)],
        20 * rows * cols,
        6 * rows * cols,
        cost=LOW,
    )(d_pairs, raw, cosine, sine, gain)


def feed(mids, cots, pieces, w_down, index, total, earlier, place):
    rows, depth = mids[0].shape
    parts = len(mids)
    hidden = w_down.shape[0]
    count = len(pieces)
    unit = place[1]
    steps = hidden // unit
    block_rows = depth // (4 * count)

    def kernel(me_ref, *refs):
        mid_refs = refs[:parts]
        cot_refs = refs[parts : 2 * parts]
        piece_refs = refs[2 * parts : 2 * parts + count]
        wd_ref = refs[2 * parts + count]
        if count > 1:
            act_ref, d_ref, wp_ref = refs[-3:]
            for which in range(4 * count):
                start = pl.multiple_of((me_ref[0] ^ which) * block_rows, block_rows)
                near = which % 4 * block_rows
                wp_ref[pl.ds(start, block_rows), :] = piece_refs[which // 4][
                    near : near + block_rows
                ]
        else:
            act_ref, d_ref = refs[-2:]
            wp_ref = piece_refs[0]
        for part in range(parts):
            now = slice(part * rows, (part + 1) * rows)
            both = mat(mid_refs[part][...], wp_ref[...])
            gate = both[:, :unit]
            up = both[:, unit:]
            d_act = dot_last(cot_refs[part][...], wd_ref[...])
            sig = 1.0 / (1.0 + jnp.exp2(gate * (-LOG2E)))
            silu = gate * sig
            act_ref[now] = (silu * up).astype(BF)
            d_ref[now, unit:] = (d_act * silu).astype(BF)
            d_ref[now, :unit] = (d_act * up * (sig + silu * (1.0 - sig))).astype(BF)

    def piece_spec(far):
        return pl.BlockSpec((pieces[0].shape[0], 2 * unit), lambda j, me: (0, j ^ far))

    out_specs = [
        pl.BlockSpec((parts * rows, unit), lambda j, me: (index, j)),
        pl.BlockSpec((parts * rows, 2 * unit), lambda j, me: (index, j)),
    ]
    out_shape = [
        jax.ShapeDtypeStruct((total * parts * rows, hidden), BF),
        jax.ShapeDtypeStruct((total * parts * rows, 2 * hidden), BF),
    ]
    if count > 1:
        out_specs.append(pl.BlockSpec((depth, 2 * unit), lambda j, me: (0, j)))
        out_shape.append(jax.ShapeDtypeStruct((depth, 2 * hidden), BF))
    before = 1 + 2 * parts + count + 1
    return call(
        kernel,
        "feed",
        (steps,),
        [fixed((rows, depth))] * parts
        + [
            pl.BlockSpec(
                (rows, depth), lambda j, me: (index, 0), pipeline_mode=pl.Buffered(1)
            )
        ]
        * parts
        + [piece_spec(which) for which in range(count)]
        + [pl.BlockSpec((unit, depth), lambda j, me: (j, 0))]
        + [pl.BlockSpec(memory_space=pl.ANY)] * len(earlier),
        out_specs,
        out_shape,
        6 * parts * rows * depth * hidden,
        2 * (2 * parts * rows * depth + 3 * depth * hidden + 3 * parts * rows * hidden),
        aliases={before + i: i for i in range(len(earlier))},
        scalars=1,
    )(place[0], *mids, *cots, *pieces, w_down, *earlier)


def feed_out(left, weight, index, parts, transposed, name, dtype=BF):
    depth = left.shape[1]
    cols = weight.shape[0] if transposed else weight.shape[1]
    rows = parts[1]

    def kernel(a_ref, w_ref, *outs):
        for part in range(parts[0]):
            now = a_ref[part * rows : (part + 1) * rows]
            result = dot_last(now, w_ref[...]) if transposed else mat(now, w_ref[...])
            outs[part][...] = result.astype(dtype)

    return call(
        kernel,
        name,
        (cols // BLOCK,),
        [
            pl.BlockSpec((parts[0] * rows, depth), lambda j: (index, 0)),
            pl.BlockSpec((BLOCK, depth), lambda j: (j, 0))
            if transposed
            else pl.BlockSpec((depth, BLOCK), lambda j: (0, j)),
        ],
        [pl.BlockSpec((rows, BLOCK), lambda j: (0, j))] * parts[0],
        [jax.ShapeDtypeStruct((rows, cols), dtype)] * parts[0],
        2 * parts[0] * rows * depth * cols,
        2 * (parts[0] * rows * (depth + cols) + depth * cols),
    )(left, weight)


def weight_terms(lefts, block, starts, width, size, rights, step, added, chunked, name, turn=0, cost=COST):
    depth = sum(left.shape[0] for left in lefts)
    cols = rights[0][0].shape[1]
    size_right = depth // len(rights)
    blocks = starts.shape[0]
    rows = blocks * size
    steps = cols // step
    nl, nr = len(lefts), len(rights)

    def kernel(block_ref, start_ref, *refs):
        left_refs = refs[:nl]
        right_refs = refs[nl : nl + nr]
        add_refs = refs[nl + nr : nl + nr + len(added)]
        out_ref, turned = refs[-2:]

        @pl.when(pl.program_id(0) == 0)
        def _():
            for which in range(blocks):
                start = pl.multiple_of(start_ref[which], 128)
                at = 0
                for ref in left_refs:
                    turned[which * size : (which + 1) * size, at : at + ref.shape[0]] = ref[
                        :, pl.ds(start, size)
                    ].T
                    at += ref.shape[0]

        right = [ref[...] for ref in right_refs]
        right = right[0] if nr == 1 else jnp.concatenate(right, axis=0)
        result = mat(turned[...], right)
        for ref in add_refs:
            result = result + ref[...].astype(F32)
        out_ref[...] = result.astype(BF)

    if chunked:
        out_spec = pl.BlockSpec((rows, step), lambda j, b, s: (j ^ turn, 0))
        shape = (steps * rows, step)
    else:
        out_spec = pl.BlockSpec((rows, step), lambda j, b, s: (0, j))
        shape = (rows, cols)
    return call(
        kernel,
        name,
        (steps,),
        [
            pl.BlockSpec(
                (left.shape[0], width), lambda j, b, s: (0, b[0]), pipeline_mode=pl.Buffered(1)
            )
            for left in lefts
        ]
        + [
            pl.BlockSpec((size_right, step), functools.partial(lambda at, j, b, s: (at, j), at))
            for right, at in rights
        ]
        + [out_spec] * len(added),
        out_spec,
        jax.ShapeDtypeStruct(shape, BF),
        2 * rows * depth * cols,
        2 * (rows * depth + depth * cols + (1 + len(added)) * rows * cols),
        scratch=[pltpu.VMEM((rows, depth), BF)],
        scalars=2,
        cost=cost,
    )(block, starts, *lefts, *[right for right, at in rights], *added)


def column_parts(gate, up, high, slots, number):
    rows, cols = gate.shape
    unit = cols // (4 * high)

    def kernel(slot_ref, gate_ref, up_ref, out_ref):
        out_ref[:, :unit] = gate_ref[...]
        out_ref[:, unit:] = up_ref[...]

    block = pl.BlockSpec((rows, unit), lambda i, j, at: (0, (at[0] ^ j) * 4 + at[i + 1]))
    return call(
        kernel,
        "column_parts",
        (number, high),
        [block, block],
        pl.BlockSpec((rows, 2 * unit), lambda i, j, at: (i, j)),
        jax.ShapeDtypeStruct((number * rows, 2 * unit * high), BF),
        0,
        8 * number * rows * unit * high,
        scalars=1,
    )(slots, gate, up)


def lay_pairs(chunks, place, high, unit):
    depth = len(chunks)
    rows = chunks[0].shape[1]
    cols = 4 * high * unit
    size = rows // 4

    def kernel(place_ref, *refs):
        gate_ref, up_ref = refs[-2:]
        for which in range(depth):
            chunk = place_ref[0] ^ which
            far = place_ref[1] ^ (chunk // 2)
            for near in range(4):
                start = pl.multiple_of((far * 4 + (place_ref[2] ^ near)) * unit, 128)

                @pl.when(chunk % 2 == 0)
                def _():
                    gate_ref[:, pl.ds(start, unit)] = refs[which][near].astype(F32)

                @pl.when(chunk % 2 == 1)
                def _():
                    up_ref[:, pl.ds(start, unit)] = refs[which][near].astype(F32)

    return call(
        kernel,
        "lay_pairs",
        (4,),
        [pl.BlockSpec((4, size, unit), lambda i, at: (0, i, 0))] * depth,
        [pl.BlockSpec((size, cols), lambda i, at: (i, 0))] * 2,
        [jax.ShapeDtypeStruct((rows, cols), F32)] * 2,
        0,
        12 * rows * cols,
        scalars=1,
    )(place, *chunks)


def visibility(parent, layout, offset, count):
    blocks = parent.shape[0]
    ident = jnp.arange(blocks, dtype=jnp.int32)
    current = ident
    reach = ident[:, None] == ident[None, :]
    for step in range(blocks):
        current = jnp.sum(jnp.where(current[:, None] == ident[None, :], parent[None, :], 0), axis=1)
        reach = reach | (current[:, None] == ident[None, :])
    place = (layout[:, None] == ident[None, :]).astype(jnp.int32)
    picked = jnp.sum(place[:, :, None] * reach.astype(jnp.int32)[None, :, :], axis=1)
    row_reach = jnp.sum(picked[:, None, :] * place[None, :, :], axis=2) > 0
    mine = lax.dynamic_slice_in_dim(row_reach, offset // BLK, count // BLK, 0).T
    spread = jnp.broadcast_to(
        mine[:, None, :, None], (blocks, BLK, count // BLK, BLK)
    ).reshape(blocks * BLK, count)
    query_rows = offset + lax.broadcasted_iota(jnp.int32, (blocks * BLK, count), 1)
    key_rows = lax.broadcasted_iota(jnp.int32, (blocks * BLK, count), 0)
    same = query_rows // BLK == key_rows // BLK
    return (spread & (jnp.logical_not(same) | (key_rows <= query_rows))).astype(F32)


def gather_small(vector, me):
    count = lax.axis_size("fsdp")
    buffer = jnp.zeros((count,) + vector.shape, vector.dtype)
    buffer = lax.dynamic_update_index_in_dim(buffer, vector, me, 0)
    step = 1
    while step < count:
        buffer = buffer + swap(buffer, step)
        step *= 2
    return buffer


def gather_rows(shard):
    high = lax.axis_size("fsdp") // 4
    return jnp.concatenate(
        [shard] + [swap(shard, 4 * far) for far in range(1, high)], axis=0
    )


def group_rows(rows):
    from_x = swap(rows, 2)
    from_core = swap(rows, 1)
    from_both = swap(from_x, 1)
    return [rows, from_core, from_x, from_both]


def group_half(parts):
    got = swap(jnp.concatenate([parts[1], parts[3]], axis=0), 1)
    rows = parts[0].shape[0]
    own = parts[0].astype(F32) + got[:rows].astype(F32)
    return own, (parts[2].astype(F32) + got[rows:].astype(F32)).astype(BF)


def gather_ctx(chunk):
    count = lax.axis_size("ctx")
    return [chunk] + [
        lax.ppermute(chunk, "ctx", [(i, i ^ step) for i in range(count)])
        for step in range(1, count)
    ]


def scatter_ctx(array):
    return lax.psum_scatter(array, "ctx", scatter_dimension=0, tiled=True)


def spread_near(piece, me):
    slot = me % 4
    rows = piece.shape[0] // 4
    near = [lax.dynamic_slice_in_dim(piece, (slot ^ which) * rows, rows, 0) for which in range(4)]
    return near, jnp.stack([near[0]] + [swap(near[which], which) for which in range(1, 4)])


def fold(value, bits, *others):
    for bit in bits:
        half = value.shape[0] // 2
        got = swap(value[half:], bit)
        keep = after(value[:half], *others) if others else value[:half]
        value = (keep.astype(F32) + got.astype(F32)).astype(BF)
        others = ()
    return value


def order_of(bits):
    order = [0]
    for bit in reversed(bits):
        order = order + [entry ^ bit for entry in order]
    return order


def body(
    inputs,
    depths,
    parents,
    layout,
    gain_attn,
    w_query,
    w_key,
    w_value,
    query_gain,
    key_gain,
    w_output,
    gain_ffn,
    w_gate,
    w_up,
    w_down,
    cotangent,
):
    me = lax.axis_index("fsdp")
    micro, local, _ = inputs.shape
    total = micro * local
    offset = lax.axis_index("ctx") * local
    count = lax.axis_size("fsdp")
    shard = D // count
    head_shard = DH // count

    def rows_of(index):
        return slice(index * local, (index + 1) * local)

    pair_shard = jnp.stack(
        [w_key.reshape(shard, KVH, DH), w_value.reshape(shard, KVH, DH)], axis=2
    ).reshape(shard, 2 * KVH * DH)
    gains = gather_small(jnp.concatenate([gain_attn, gain_ffn, query_gain, key_gain]), me)
    w_qkv = lax.all_gather(
        jnp.concatenate([w_query, pair_shard], axis=1), "fsdp", axis=0, tiled=True
    )
    attn_gain = gains[:, :shard].reshape(D).astype(F32)
    ffn_gain = gains[:, shard : 2 * shard].reshape(D).astype(F32)
    q_gain = gains[:, 2 * shard : 2 * shard + head_shard].reshape(1, DH).astype(F32)
    k_gain = gains[:, 2 * shard + head_shard :].reshape(1, DH).astype(F32)

    unit = FF // count
    high = count // 4
    slot = me % 4
    parts_x = column_parts(w_gate, w_up, high, jnp.stack([me // 4, slot ^ 2, slot ^ 3]), 2)
    parts_own = column_parts(
        after(w_gate, parts_x), w_up, high, jnp.stack([me // 4, slot, slot ^ 1]), 2
    )
    got_x = swap(after(parts_x, w_qkv, gains), 2)
    wd = gather_rows(after(w_down, w_qkv, gains))
    out_pieces = [w_output]
    out_order = [0]
    bit = count // 2
    while bit > 2:
        out_pieces += [swap(piece, bit) for piece in out_pieces]
        out_order += [entry ^ bit for entry in out_order]
        bit //= 2
    out_block = jnp.concatenate(out_pieces, axis=0)
    cot_all = cotangent.reshape(total, D)

    freq = jnp.power(BASE, -jnp.arange(DH // 2, dtype=F32) / (DH // 2))
    angle = depths.reshape(total).astype(F32)[:, None] * freq[None, :]
    cosine = jnp.cos(angle)
    sine = jnp.sin(angle)
    cosine = jnp.concatenate([cosine, cosine], axis=1)
    sine = jnp.concatenate([-sine, sine], axis=1)
    masks = [
        visibility(parents[index, 0], layout[index, 0], offset, local) for index in range(micro)
    ]

    source = inputs.reshape(total, D).astype(F32)
    inv_in = inv_rms(source)
    normed_b = (source * inv_in * attn_gain).astype(BF)
    normed_now = after(normed_b, parts_own, out_block, *masks)
    pairs, pairs_raw = project(
        normed_now,
        w_qkv,
        QH * DH,
        2 * KVH * DH,
        cosine,
        sine,
        k_gain,
        "r-r-",
        "project_pairs",
    )
    everyone = [
        lax.all_gather(pairs[rows_of(index)], "ctx", axis=0, tiled=True) for index in range(micro)
    ]
    got_core = swap(
        jnp.concatenate([parts_own[shard:], after(got_x, pairs, wd)[shard:]], axis=0), 1
    )
    near = jnp.concatenate(
        [parts_own[:shard], got_core[:shard], got_x[:shard], got_core[shard:]], axis=0
    )
    queries, queries_raw = project(
        after(normed_b, pairs, near, wd),
        w_qkv,
        0,
        QH * DH,
        cosine,
        sine,
        q_gain,
        "rrrr",
        "project_queries",
        0.01,
    )
    pieces = [near] + [swap(near, 4 * far) for far in range(1, high)]
    for bit, earlier in ((2, near), (1, everyone[0])):
        out_block = jnp.concatenate([out_block, swap(after(out_block, earlier), bit)], axis=0)
        out_order = out_order + [entry ^ bit for entry in out_order]
    w_out = jnp.zeros((QH * DH, D), BF)
    for index, entry in enumerate(out_order):
        w_out = lax.dynamic_update_slice_in_dim(
            w_out, out_block[index * shard : (index + 1) * shard], (me ^ entry) * shard, 0
        )
    cot_x = swap(after(cot_all, near), 2)
    cot_rows = [cot_all, swap(cot_all, 1), cot_x, swap(cot_x, 1)]

    attended = []
    inverses = []
    middles = []
    mid_inverses = []
    mid_rows = []
    token = queries
    for index in range(micro):
        part = rows_of(index)
        if index == 0:
            token = (token,)
        else:
            token = (token, cot_x)
        out, inverse = attention(after(queries[part], *token), everyone[index], masks[index])
        middle = source[part] + mat(after(out, w_out) if index == 0 else out, w_out)
        inv_mid = inv_rms(middle)
        mid_b = (middle * inv_mid * ffn_gain).astype(BF)
        attended.append(out)
        inverses.append(inverse)
        middles.append(middle)
        mid_inverses.append(inv_mid)
        mid_rows.append(group_rows(mid_b))
        token = mid_b

    mid_pieces = [piece for rows in mid_rows for piece in rows]
    cot_pieces = [(piece, index) for index in range(micro) for piece in cot_rows]
    zero = jnp.zeros((1,), jnp.int32)

    def down_terms(act, far, added, cost=COST):
        return weight_terms(
            [act],
            zero + far,
            zero,
            unit,
            unit,
            cot_pieces,
            BLOCK,
            added,
            False,
            "grad_down",
            cost=cost,
        )

    def pair_terms(first, far, added, cost=COST):
        return weight_terms(
            [first] + mid_pieces[1:],
            ((me // 4) ^ far)[None],
            zero,
            D // high,
            D // high,
            [(dgu_b, 0)],
            unit,
            added,
            True,
            "grad_pair",
            2 * far,
            cost,
        )

    d_mids = []
    me_array = me[None]
    act_b, dgu_b, wgu = feed(
        [after(mid_rows[0][0], token)] + mid_rows[0][1:],
        cot_rows,
        pieces,
        wd,
        0,
        micro,
        (),
        (me_array, unit),
    )
    for index in range(micro):
        if index:
            act_b, dgu_b = feed(
                [after(mid_rows[index][0], token)] + mid_rows[index][1:],
                cot_rows,
                [wgu],
                wd,
                index,
                micro,
                (act_b, dgu_b),
                (me_array, unit),
            )
        parts = feed_out(
            after(dgu_b, act_b, *[d_mid[1] for d_mid in d_mids]),
            wgu,
            index,
            (4, local),
            True,
            "feed_back",
        )
        d_mids.append(group_half(parts))
        token = parts[0]
    sent_pair = []
    for far in range(1, high):
        sent_pair.append(pair_terms(after(mid_pieces[0], token), far, []))
        token = sent_pair[-1]
    got_pair = [swap(piece, 4 * (far + 1)) for far, piece in enumerate(sent_pair)]

    d_middles = []
    d_projs = []
    d_query_parts = []
    d_pair_parts = []
    d_ffn_gain = jnp.zeros((D,), F32)
    d_q_gain = jnp.zeros((1, DH), F32)
    for index in range(micro):
        part = rows_of(index)
        d_mid = d_mids[index][0] + swap(d_mids[index][1], 2).astype(F32)
        d_part, d_gain = rms_back(
            middles[index], mid_inverses[index], ffn_gain, after(d_mid, token)
        )
        d_ffn_gain = d_ffn_gain + d_gain
        d_middle = cotangent[index].astype(F32) + d_part
        d_proj = d_middle.astype(BF)
        d_attended = dot_last(d_proj, w_out).astype(BF)
        d_query, d_pair, d_gain = attention_back(
            after(queries[part], *[d_mids[later][1] for later in range(index + 1, micro)]),
            queries_raw[part],
            everyone[index],
            masks[index],
            d_attended,
            attended[index],
            inverses[index],
            cosine[part],
            sine[part],
            q_gain,
        )
        d_q_gain = d_q_gain + d_gain
        d_middles.append(d_middle)
        d_projs.append(d_proj)
        d_query_parts.append(d_query)
        d_pair_parts.append(scatter_ctx(d_pair))
        token = d_query
        if index == micro - 1:
            sent_down = []
            for far in range(1, high):
                sent_down.append(down_terms(after(act_b, token), far, []))
                token = sent_down[-1]
            got_down = [swap(piece, 4 * (far + 1)) for far, piece in enumerate(sent_down)]

    d_query_b = jnp.concatenate(d_query_parts, axis=0)
    d_proj_b = jnp.concatenate(d_projs, axis=0)
    attended_b = jnp.concatenate(attended, axis=0)
    bits = [2**i for i in range(count.bit_length() - 1)]
    half_size = count // 2

    def plain_terms(left, right, order, added, name, cost=COST):
        starts = (me ^ jnp.array(order, jnp.int32)) * shard
        return weight_terms(
            [left], zero, starts, D, shard, [(right, 0)], BLOCK, added, False, name, cost=cost
        )

    order = order_of(bits)
    out_parts = []
    for index in range(micro):
        out_parts.append(
            feed_out(after(act_b, token), wd, index, (4, local), False, "feed_forward")
        )
        token = out_parts[-1][0]
    out_half = group_half([jnp.concatenate(list(pair), axis=0) for pair in zip(*out_parts)])
    sent_query = plain_terms(after(normed_b, token), d_query_b, order[half_size:], [], "grad_q")
    sent_output = plain_terms(
        after(attended_b, sent_query), d_proj_b, order[half_size:], [], "grad_o"
    )
    own_pair = pair_terms(after(mid_pieces[0], sent_output, out_half[1]), 0, got_pair)
    own_query = plain_terms(
        after(normed_b, own_pair), d_query_b, order[:half_size], [swap(sent_query, 1)], "grad_q"
    )
    own_output = plain_terms(
        after(attended_b, own_query), d_proj_b, order[:half_size], [swap(sent_output, 1)], "grad_o"
    )
    own_down = down_terms(after(act_b, own_output), 0, got_down)
    outputs = jnp.concatenate(middles, axis=0) + out_half[0]
    outputs = (outputs + swap(out_half[1], 2).astype(F32)).astype(BF).reshape(micro, local, D)
    pair_piece = scatter_ctx(own_pair)
    down_piece = scatter_ctx(after(own_down, own_pair))

    d_pairs = after(jnp.concatenate(d_pair_parts, axis=0), own_down, outputs)
    d_pair_b, d_k_gain = pair_back(d_pairs, pairs_raw, cosine, sine, k_gain)
    part_qo = [fold(own_query, bits[1:2], d_pair_b), fold(own_output, bits[1:2], d_pair_b)]
    sent_kv = plain_terms(after(normed_b, *part_qo), d_pair_b, order[half_size:], [], "grad_kv", LOW)
    (d_normed,) = feed_out(
        jnp.concatenate([after(d_query_b, sent_kv), d_pair_b], axis=1),
        w_qkv,
        0,
        (1, total),
        True,
        "d_normed",
        F32,
    )
    own_kv = plain_terms(
        after(normed_b, d_normed), d_pair_b, order[:half_size], [swap(sent_kv, 1)], "grad_kv"
    )
    d_source, d_attn_gain = rms_back(source, inv_in, attn_gain, after(d_normed, own_kv))
    grad_inputs = jnp.concatenate(d_middles, axis=0) + d_source

    def spread(vector):
        return jnp.pad(vector.reshape(count, -1), ((0, 0), (0, shard - vector.size // count)))

    columns = jnp.stack(
        [
            d_attn_gain.reshape(count, shard),
            d_ffn_gain.reshape(count, shard),
            spread(d_q_gain),
            spread(d_k_gain),
        ],
        axis=2,
    ).astype(BF)
    columns = jnp.pad(columns, ((0, 0), (0, 0), (0, DH - 4))).reshape(D, DH)
    columns = jnp.concatenate(
        [
            lax.dynamic_slice_in_dim(columns, (me ^ entry) * shard, shard, 0)
            for entry in order
        ],
        axis=0,
    )
    columns = fold(columns, bits[:1])
    near_parts, pair_near = spread_near(pair_piece, me)
    chunks = gather_ctx(pair_near)
    down_whole = lax.all_gather(down_piece, "ctx", axis=0, tiled=True)
    part_qo = fold(jnp.concatenate(part_qo, axis=1), bits[2:])
    part_kv = fold(
        jnp.concatenate([after(own_kv, *near_parts), columns], axis=1), bits[1:2], pair_near
    )
    part_kv = fold(part_kv, bits[2:])

    grad_gate, grad_up = lay_pairs(
        chunks, jnp.stack([lax.axis_index("ctx"), me // 4, slot]), high, unit
    )

    def whole(piece):
        return lax.all_gather(after(piece, *chunks[1:]), "ctx", axis=0, tiled=True).astype(F32)

    grad_down = down_whole.astype(F32)
    both = whole(scatter_ctx(part_qo))
    grad_query, grad_output = both[:, :D], both[:, D:]
    rest = whole(scatter_ctx(part_kv))
    pair_both = rest[:, : 2 * KVH * DH].reshape(shard, KVH, 2, DH)
    grad_key = pair_both[:, :, 0].reshape(shard, KVH * DH)
    grad_value = pair_both[:, :, 1].reshape(shard, KVH * DH)
    sums = rest[:, 2 * KVH * DH :]

    return (
        outputs,
        grad_inputs.reshape(micro, local, D),
        sums[:, 0],
        grad_query,
        grad_key,
        grad_value,
        sums[:head_shard, 2],
        sums[:head_shard, 3],
        grad_output,
        sums[:, 1],
        grad_gate,
        grad_up,
        grad_down,
    )


def solution(mesh):
    rows = P(None, ("fsdp", "ctx"), None)
    tree = P(None, "fsdp", None)
    vector = P("fsdp")
    weight = P("fsdp", None)
    in_specs = (
        rows,
        P(None, ("fsdp", "ctx")),
        tree,
        tree,
        vector,
        weight,
        weight,
        weight,
        vector,
        vector,
        weight,
        vector,
        weight,
        weight,
        weight,
        rows,
    )
    out_specs = (
        rows,
        rows,
        vector,
        weight,
        weight,
        weight,
        vector,
        vector,
        weight,
        vector,
        weight,
        weight,
        weight,
    )
    return jax.shard_map(body, mesh=mesh, in_specs=in_specs, out_specs=out_specs, check_vma=False)
```
